32 devices in a mesh: tile: 8 (over z, y), frame: 4 (over x, core).
Axes of the slice: x: 2, y: 2, z: 4, core: 2. Of those that a mesh axis runs over, the one named last changes fastest.
Arguments:
- movie: bfloat16 [32, 512, 256], P(('frame', 'tile')), may hold values from -6 to 6
- footprints: bfloat16 [512, 256, 384], P('tile'), may hold values from -0.09375 to 0.09375
- support: int32 [64, 384], P('tile'), may hold values 0 or 1
- traces: bfloat16 [3072, 32], P('tile', 'frame'), may hold values from 0 to 2
- border_weight: float32 [512, 256], P('tile'), may hold values from 1 to 4
- border_offsets: int32 [64, 2], replicated, may hold values from -16 to 16, as said below
Outputs:
- new_traces: float32 [3072, 32], P('tile', 'frame')
- trace_gram: float32 [3072, 384], P('tile')
- remainder: bfloat16 [32, 512, 256], P(('frame', 'tile'))
The draws below stay inside these ranges and needn't reach their ends.
Inputs may be any that keep to these rules, and one draw needn't show every extreme that they name: `border_offsets`: the 64 rows are distinct offsets (row, column) on the boundary of the square of half-side 16; (-16, -16) and (16, 16) are among them.
All inputs are finite; a program needn't handle non-finite values. No bound on the sum of `support` on one device may be relied on, other than what follows from the above.
Results may differ from the reference program's by a relative error of at most 0.009.
Values may be sent and summed in bfloat16 or wider, within the bound.
No kernel may reach another device: no remote copies, remote signals or barrier semaphores. Data moves between devices by JAX's collectives and lax.ppermute only.
A program may use at most 128 MiB of HBM per device.

```python
import math
import jax
import jax.numpy as jnp
import numpy as np
from jax import lax

TH = 64
W = 256
KT = 384
RR = 16
GR = 4
BR = 8
SWEEPS = 3
NR = 64
H = 512
K = 3072
FRAMES = 32
N_TILE = 8


def draw_border_offsets(key, part):
    perimeter = 8 * RR
    remaining = np.concatenate([np.arange(1, 4 * RR), np.arange(4 * RR + 1, perimeter)]).astype(np.int32)
    shuffled = jax.random.permutation(key, perimeter - 2)
    chosen = jnp.concatenate([jnp.array([0, 4 * RR], jnp.int32), jnp.asarray(remaining)[shuffled[:NR - 2]]])
    which_side = chosen // (2 * RR)
    position = chosen % (2 * RR) - RR
    offset_rows = jnp.where(which_side == 0, -RR, jnp.where(which_side == 1, position, jnp.where(which_side == 2, RR, -position)))
    offset_cols = jnp.where(which_side == 0, position, jnp.where(which_side == 1, RR, jnp.where(which_side == 2, -position, -RR)))
    return jnp.stack([offset_rows, offset_cols], axis=1).astype(jnp.int32)


def set_ends(values, rng, least, top_value):
    longest = values.shape.index(max(values.shape))
    spots = []
    for shift in (0, 1):
        where = [jax.random.randint(jax.random.fold_in(rng, axis), (), 0, length) for axis, length in enumerate(values.shape)]
        where[longest] = (where[longest] + shift) % values.shape[longest]
        spots.append(tuple(where))
    return values.at[spots[0]].set(least).at[spots[1]].set(top_value)


def block_scale(own_key, dims, split, smallest, high):
    def one(axis_at, parts):
        heights = jax.random.uniform(jax.random.fold_in(jax.random.fold_in(own_key, 6), axis_at), (parts,), jnp.float32, smallest / len(split), high / len(split))
        return jnp.repeat(jnp.exp(heights), dims[axis_at] // parts).reshape((-1,) + (1,) * (len(dims) - axis_at - 1))

    loudness = one(*split[0])
    for cut in split[1:]:
        loudness = loudness * one(*cut)
    return loudness


def gaussian(own_key, shape, scale, bound, shards=(), kind=jnp.bfloat16):
    factor_of = block_scale(own_key, shape, shards, -0.22, 0.18) if shards else 1.0
    result = jax.random.normal(own_key, shape, jnp.float32) * scale * factor_of
    return jnp.minimum(jnp.maximum(result, -bound), bound).astype(kind)


def setup_inputs(seed: int = 0) -> dict:
    streams_of = jax.random.split(jax.random.key(seed), 7)
    movie = gaussian(streams_of[0], (FRAMES, H, W), 1.0, 6.0, ((0, 32),))
    footprints = gaussian(streams_of[1], (H, W, KT), (TH * W // 4) ** -0.5, 0.09375, ((0, 8),))
    support = set_ends((jax.random.randint(streams_of[2], (H // BR, KT), 0, 2) < 1).astype(jnp.int32), jax.random.fold_in(streams_of[2], 1), 0, 1)
    traces = jnp.clip(2.0 * jax.random.uniform(streams_of[3], (K, FRAMES), jnp.float32) ** block_scale(streams_of[3], (K, FRAMES), ((0, 8), (1, 4)), -0.2, 0.2), 0.0, 2.0).astype(jnp.bfloat16)
    border_weight = jnp.clip(jnp.exp(math.log(4.0) - 1.3862944 * jax.random.uniform(streams_of[4], (H, W), jnp.float32) ** block_scale(streams_of[4], (H, W), ((0, 8),), -0.2, 0.2)), 1.0, 4.0)
    border_offsets = draw_border_offsets(jax.random.fold_in(streams_of[6], 71), 0)
    return dict(movie=movie, footprints=footprints, support=support, traces=traces, border_weight=border_weight, border_offsets=border_offsets)


def gaussian_taps(radius):
    spots = jnp.arange(-radius, radius + 1).astype(jnp.float32)
    raw_weights = jnp.exp(-2.0 * spots * spots / float(radius * radius))
    return raw_weights / jnp.sum(raw_weights)

def smooth_along(values_in, taps_table, radius, along_axis):
    extent = values_in.shape[along_axis]
    pad_widths = [(0, 0)] * values_in.ndim
    pad_widths[along_axis] = (radius, radius)
    padded = jnp.pad(values_in, pad_widths)
    running = jnp.zeros(values_in.shape, jnp.float32)
    for offset_step in range(2 * radius + 1):
        running = running + taps_table[offset_step] * lax.slice_in_dim(padded, offset_step, offset_step + extent, axis=along_axis)
    return running

def reference(movie, footprints, support, traces, border_weight, border_offsets):
    frames_all = movie.shape[0]
    pixel_count = TH * W
    block_masks = jnp.repeat(support, BR, axis=0).astype(jnp.bfloat16)
    shaped = (footprints * block_masks[:, None, :]).reshape(N_TILE, pixel_count, KT)
    grouped = traces.reshape(N_TILE, KT, frames_all)
    pixels = movie.reshape(frames_all, N_TILE, pixel_count).transpose(1, 0, 2)

    def activity(operands):
        strip_fp, strip_tr = operands
        return jnp.einsum('kf,pk->fp', strip_tr, strip_fp, preferred_element_type=jnp.float32)
    fitted = lax.map(activity, (shaped, grouped))
    first = (pixels.astype(jnp.float32) - fitted).astype(jnp.bfloat16)
    image = first.transpose(1, 0, 2).reshape(frames_all, H, W)
    taps_table = gaussian_taps(GR)
    smooth = smooth_along(smooth_along(image.astype(jnp.float32), taps_table, GR, 1), taps_table, GR, 2).astype(jnp.bfloat16)
    padded = jnp.pad(smooth.astype(jnp.float32), ((0, 0), (RR, RR), (RR, RR)))
    zero_index = jnp.zeros((), jnp.int32)

    def add_offset(offset_step, running):
        row_start = (border_offsets[offset_step, 0] + RR).astype(jnp.int32)
        col_start = (border_offsets[offset_step, 1] + RR).astype(jnp.int32)
        return running + lax.dynamic_slice(padded, (zero_index, row_start, col_start), (frames_all, H, W))
    summed = lax.fori_loop(0, NR, add_offset, jnp.zeros((frames_all, H, W), jnp.float32))
    background = border_weight[None, :, :] * summed / math.sqrt(NR)
    cleaned = (movie.astype(jnp.float32) - background).astype(jnp.bfloat16)
    cleaned_strips = cleaned.reshape(frames_all, N_TILE, pixel_count).transpose(1, 0, 2)

    def temporal(operands):
        strip_fp, strip_tr, strip_data = operands
        projected = jnp.einsum('pk,fp->kf', strip_fp, strip_data, preferred_element_type=jnp.float32)
        coupling = jnp.einsum('pk,pq->kq', strip_fp, strip_fp, preferred_element_type=jnp.float32)
        floor_t = jnp.maximum(jnp.diagonal(coupling), 1.0)
        trace_state = strip_tr.astype(jnp.float32)
        for sweep_index in range(SWEEPS):
            moved = jnp.dot(coupling, trace_state, precision=lax.Precision.HIGHEST)
            trace_state = jnp.maximum(trace_state + (projected - moved) / floor_t[:, None], 0.0)
        gram_block = jnp.dot(trace_state, trace_state.T, precision=lax.Precision.HIGHEST)
        rounded = trace_state.astype(jnp.bfloat16)
        refit = jnp.einsum('kf,pk->fp', rounded, strip_fp, preferred_element_type=jnp.float32)
        leftover = (strip_data.astype(jnp.float32) - refit).astype(jnp.bfloat16)
        return (trace_state, gram_block, leftover)
    new_traces, trace_gram, leftover = lax.map(temporal, (shaped, grouped, cleaned_strips))
    remainder = leftover.transpose(1, 0, 2).reshape(frames_all, H, W)
    return (new_traces.reshape(N_TILE * KT, frames_all), trace_gram.reshape(N_TILE * KT, KT), remainder)
```

```python
import functools
import math

import jax
import jax.numpy as jnp
import numpy as np
from jax import lax
from jax.experimental import pallas as pl
from jax.experimental.pallas import tpu as pltpu
from jax.sharding import PartitionSpec as P

RR = 16
GR = 4
BR = 8
SWEEPS = 3
NR = 64
HALO = 24
LANES = 128
VMEM = pl.BlockSpec(memory_space=pltpu.VMEM)
SMEM = pl.BlockSpec(memory_space=pltpu.SMEM)


def split_high_low(values):
    high = values.astype(jnp.bfloat16)
    low = (values - high.astype(jnp.float32)).astype(jnp.bfloat16)
    return high, low


def filter_bands(tile_rows, columns):
    spots = np.arange(-GR, GR + 1).astype(np.float32)
    raw = np.exp(np.float32(-2.0) * spots * spots / np.float32(GR * GR)).astype(np.float32)
    taps = (raw / raw.sum(dtype=np.float32)).astype(np.float32)

    def band(count_out, count_in, shift):
        distance = np.arange(count_in)[None, :] - np.arange(count_out)[:, None] - shift
        inside = np.abs(distance) <= GR
        return np.where(inside, taps[np.clip(distance + GR, 0, 2 * GR)], np.float32(0.0))

    def parts(matrix):
        high = matrix.astype(jnp.bfloat16)
        low = (matrix - high.astype(np.float32)).astype(jnp.bfloat16)
        return high, low

    rows_high, rows_low = parts(band(tile_rows + 2 * RR, tile_rows + 2 * HALO, HALO - RR))
    cols_high, cols_low = parts(band(columns, columns, 0))
    return (
        jnp.asarray(np.concatenate([rows_high, rows_low], axis=1)),
        jnp.asarray(np.concatenate([cols_high, cols_high, cols_low], axis=0)),
    )


def border_tables(offsets_ref, table_ref, sides_ref):
    columns = table_ref.shape[1]
    tile_rows = sides_ref.shape[0] // 2
    places = lax.broadcasted_iota(jnp.int32, (8, columns), 0) * columns + lax.broadcasted_iota(
        jnp.int32, (8, columns), 1
    )
    base = jnp.zeros((8, columns), jnp.float32)
    for entry in range(offsets_ref.shape[1]):
        row = offsets_ref[0, entry]
        col = offsets_ref[1, entry]
        along_top = row == -RR
        along_row = along_top | (row == RR)
        first_lane = jnp.where(col > 0, columns - col, -col)
        kind = jnp.where(along_row, jnp.where(along_top, 0, 1), jnp.where(col < 0, 2, 3))
        lane = jnp.where(along_row, first_lane, row + RR)
        base = base + jnp.where(places == kind * columns + lane, 1.0, 0.0)
    distance = lax.broadcasted_iota(jnp.int32, (columns, columns), 0) - lax.broadcasted_iota(
        jnp.int32, (columns, columns), 1
    )
    near = jnp.abs(distance) <= RR
    for kind in range(2):
        spread = jnp.broadcast_to(base[kind : kind + 1, :], (columns, columns))
        turned = pltpu.roll(spread, 0, 1, stride=1, stride_axis=0)
        table_ref[kind * columns : (kind + 1) * columns, :] = jnp.where(near, turned, 0.0).astype(
            jnp.bfloat16
        )
    width = sides_ref.shape[1]
    for kind in range(2):
        spread = jnp.broadcast_to(base[2 + kind : 3 + kind, :width], (tile_rows, width))
        turned = pltpu.roll(spread, 0, 1, stride=1, stride_axis=0)
        sides_ref[kind * tile_rows : (kind + 1) * tile_rows, :] = turned.astype(jnp.bfloat16)


def kernel_components(
    footprints_ref,
    support_ref,
    traces_ref,
    offsets_ref,
    fitted_ref,
    edge_a_ref,
    edge_b_ref,
    coupling_ref,
    turned_ref,
    table_ref,
    sides_ref,
    lined_ref,
):
    tile_rows, columns, components = footprints_ref.shape
    frames = traces_ref.shape[0]
    halves = columns // LANES
    block = BR * columns
    split = components // 256 * 256
    traces = traces_ref[...]
    for b in range(tile_rows // BR):
        mask = support_ref[b : b + 1, :].astype(jnp.bfloat16)
        shaped = footprints_ref[b * BR : (b + 1) * BR].reshape(block, components) * mask
        turned_ref[:, b * block : (b + 1) * block] = shaped.T
        turned = turned_ref[:, b * block : (b + 1) * block]
        fitted = jnp.dot(traces, turned, preferred_element_type=jnp.float32)
        for row in range(BR):
            for half in range(halves):
                start = row * columns + half * LANES
                lined_ref[half, pl.ds(b * BR + row, frames, stride=tile_rows), :] = fitted[
                    :, start : start + LANES
                ]
        left = jnp.dot(turned, shaped[:, :split], preferred_element_type=jnp.float32)
        right = jnp.dot(turned[split:], shaped[:, split:], preferred_element_type=jnp.float32)
        if b == 0:
            coupling_ref[:, :split] = left
            coupling_ref[split:, split:] = right
        else:
            coupling_ref[:, :split] += left
            coupling_ref[split:, split:] += right
    coupling_ref[:split, split:] = coupling_ref[split:, :split].T
    odd = lax.axis_index("tile") % 2 == 1
    for half in range(halves):
        lanes = slice(half * LANES, (half + 1) * LANES)
        for frame in range(frames):
            lines = lined_ref[half, frame * tile_rows : (frame + 1) * tile_rows, :]
            fitted_ref[frame, :, lanes] = lines
            top = lines[:HALO]
            bottom = lines[tile_rows - HALO :]
            edge_a_ref[frame, :, lanes] = jnp.where(odd, top, bottom).astype(jnp.bfloat16)
            edge_b_ref[frame, :, lanes] = jnp.where(odd, bottom, top).astype(jnp.bfloat16)
    border_tables(offsets_ref, table_ref, sides_ref)


def kernel_frames(
    tile_count,
    movie_ref,
    fitted_ref,
    edge_a_ref,
    edge_b_ref,
    footprints_ref,
    support_ref,
    traces_ref,
    weight_ref,
    coupling_ref,
    turned_ref,
    table_ref,
    sides_ref,
    row_filter_ref,
    col_filter_ref,
    new_traces_ref,
    rounded_ref,
    remainder_ref,
    cleaned_ref,
    refit_ref,
):
    tile_rows, columns, components = footprints_ref.shape
    frames = traces_ref.shape[0]
    halves = columns // LANES
    span = tile_rows + 2 * RR
    tile = lax.axis_index("tile")
    odd = tile % 2 == 1

    row_number = tile * tile_rows - RR + lax.broadcasted_iota(jnp.int32, (span, 1), 0)
    inside = (row_number >= 0) & (row_number < tile_count * tile_rows)
    row_filter = jnp.where(inside, row_filter_ref[...].astype(jnp.float32), 0.0).astype(
        jnp.bfloat16
    )
    tall = []
    for frame in range(frames):
        edge_a = edge_a_ref[frame].astype(jnp.float32)
        edge_b = edge_b_ref[frame].astype(jnp.float32)
        fitted = jnp.concatenate(
            [
                jnp.where(odd, edge_a, edge_b),
                fitted_ref[frame],
                jnp.where(odd, edge_b, edge_a),
            ],
            axis=0,
        )
        first = (movie_ref[frame].astype(jnp.float32) - fitted).astype(jnp.bfloat16)
        tall.append(
            jnp.dot(
                row_filter,
                jnp.concatenate([first, first], axis=0),
                preferred_element_type=jnp.float32,
            )
        )
    high, low = split_high_low(jnp.concatenate(tall, axis=0))
    smooth = jnp.dot(
        jnp.concatenate([high, low, high], axis=1),
        col_filter_ref[...],
        preferred_element_type=jnp.float32,
    ).astype(jnp.bfloat16)
    sides = sides_ref[:, :span]
    lane = lax.broadcasted_iota(jnp.int32, (tile_rows, columns), 1)
    weight = weight_ref[...]
    for frame in range(frames):
        lines = smooth[frame * span : (frame + 1) * span]
        ends = jnp.concatenate([lines[:tile_rows], lines[2 * RR :]], axis=1)
        summed = jnp.dot(ends, table_ref[...], preferred_element_type=jnp.float32)
        mixed = jnp.dot(sides, lines, preferred_element_type=jnp.float32)
        west = pltpu.roll(mixed[:tile_rows], RR, 1)
        east = pltpu.roll(mixed[tile_rows:], columns - RR, 1)
        summed = summed + jnp.where(lane >= RR, west, 0.0)
        summed = summed + jnp.where(lane < columns - RR, east, 0.0)
        background = weight * summed * (1.0 / math.sqrt(NR))
        movie = movie_ref[frame, HALO : HALO + tile_rows, :].astype(jnp.float32)
        cleaned = (movie - background).astype(jnp.bfloat16).astype(jnp.float32)
        for half in range(halves):
            cleaned_ref[half, frame * tile_rows : (frame + 1) * tile_rows, :] = cleaned[
                :, half * LANES : (half + 1) * LANES
            ]

    projected = jnp.zeros((frames, components), jnp.float32)
    for b in range(tile_rows // BR):
        part = jnp.zeros((frames, components), jnp.float32)
        for row in range(b * BR, (b + 1) * BR):
            pixels = jnp.concatenate(
                [
                    cleaned_ref[half, pl.ds(row, frames, stride=tile_rows), :]
                    for half in range(halves)
                ],
                axis=1,
            ).astype(jnp.bfloat16)
            part = part + jnp.dot(
                pixels, footprints_ref[row], preferred_element_type=jnp.float32
            )
        projected = projected + part * support_ref[b : b + 1, :].astype(jnp.float32)

    coupling = coupling_ref[...]
    diagonal = lax.broadcasted_iota(jnp.int32, coupling.shape, 0) == lax.broadcasted_iota(
        jnp.int32, coupling.shape, 1
    )
    floor = jnp.maximum(
        jnp.sum(jnp.where(diagonal, coupling, 0.0), axis=0, keepdims=True), 1.0
    )
    coupling_high, coupling_low = split_high_low(coupling)
    state = traces_ref[...].astype(jnp.float32)
    for _ in range(SWEEPS):
        state_high, state_low = split_high_low(state)
        by_high = jnp.dot(
            jnp.concatenate([state_high, state_low], axis=0),
            coupling_high,
            preferred_element_type=jnp.float32,
        )
        by_low = jnp.dot(state_high, coupling_low, preferred_element_type=jnp.float32)
        moved = by_high[:frames] + (by_high[frames:] + by_low)
        state = jnp.maximum(state + (projected - moved) / floor, 0.0)
    rounded = state.astype(jnp.bfloat16)
    new_traces_ref[...] = state
    rounded_ref[...] = rounded

    block = BR * columns
    for b in range(tile_rows // BR):
        refit = jnp.dot(
            rounded,
            turned_ref[:, b * block : (b + 1) * block],
            preferred_element_type=jnp.float32,
        )
        for row in range(BR):
            for half in range(halves):
                start = row * columns + half * LANES
                refit_ref[half, pl.ds(b * BR + row, frames, stride=tile_rows), :] = refit[
                    :, start : start + LANES
                ]
    for frame in range(frames):
        rows = slice(frame * tile_rows, (frame + 1) * tile_rows)
        for half in range(halves):
            remainder_ref[frame, :, half * LANES : (half + 1) * LANES] = (
                cleaned_ref[half, rows, :] - refit_ref[half, rows, :]
            ).astype(jnp.bfloat16)


def per_device(movie, footprints, support, traces, border_weight, border_offsets):
    tile_count = lax.axis_size("tile")
    tile_rows, columns, components = footprints.shape
    own_frames = movie.shape[0]
    frames = own_frames * tile_count
    pixels = tile_rows * columns
    halves = columns // LANES
    span = tile_rows + 2 * RR
    extended = tile_rows + 2 * HALO

    padded = jnp.pad(movie, ((0, 0), (HALO, HALO), (0, 0)))
    pieces = jnp.concatenate(
        [
            lax.slice_in_dim(padded, t * tile_rows, t * tile_rows + extended, axis=1)
            for t in range(tile_count)
        ],
        axis=0,
    )
    strip_movie = lax.all_to_all(pieces, "tile", split_axis=0, concat_axis=0, tiled=True)

    traces_rows = traces.T
    fitted, edge_a, edge_b, coupling, turned, table, sides = pl.pallas_call(
        kernel_components,
        out_shape=[
            jax.ShapeDtypeStruct((frames, tile_rows, columns), jnp.float32),
            jax.ShapeDtypeStruct((frames, HALO, columns), jnp.bfloat16),
            jax.ShapeDtypeStruct((frames, HALO, columns), jnp.bfloat16),
            jax.ShapeDtypeStruct((components, components), jnp.float32),
            jax.ShapeDtypeStruct((components, pixels), jnp.bfloat16),
            jax.ShapeDtypeStruct((2 * columns, columns), jnp.bfloat16),
            jax.ShapeDtypeStruct((2 * tile_rows, LANES), jnp.bfloat16),
        ],
        in_specs=[VMEM, VMEM, VMEM, SMEM],
        out_specs=[VMEM] * 7,
        scratch_shapes=[pltpu.VMEM((halves, frames * tile_rows, LANES), jnp.float32)],
        compiler_params=pltpu.CompilerParams(vmem_limit_bytes=12 << 20),
        cost_estimate=pl.CostEstimate(
            flops=2 * pixels * components * components,
            bytes_accessed=4 * pixels * components,
            transcendentals=0,
        ),
        name="components",
    )(footprints, support, traces_rows, border_offsets.T)

    evens = [(i, i + 1) for i in range(0, tile_count - 1, 2)]
    odds = [(i, i + 1) for i in range(1, tile_count - 1, 2)]
    edge_a = lax.ppermute(edge_a, "tile", evens + [(j, i) for i, j in evens])
    edge_b = lax.ppermute(edge_b, "tile", odds + [(j, i) for i, j in odds])

    row_filter, col_filter = filter_bands(tile_rows, columns)
    new_traces, rounded, leftover = pl.pallas_call(
        functools.partial(kernel_frames, tile_count),
        out_shape=[
            jax.ShapeDtypeStruct((frames, components), jnp.float32),
            jax.ShapeDtypeStruct((frames, components), jnp.bfloat16),
            jax.ShapeDtypeStruct((frames, tile_rows, columns), jnp.bfloat16),
        ],
        in_specs=[VMEM] * 14,
        out_specs=[VMEM] * 3,
        scratch_shapes=[pltpu.VMEM((halves, frames * tile_rows, LANES), jnp.float32)] * 2,
        compiler_params=pltpu.CompilerParams(vmem_limit_bytes=16 << 20),
        cost_estimate=pl.CostEstimate(
            flops=8 * frames * pixels * components,
            bytes_accessed=4 * pixels * components,
            transcendentals=0,
        ),
        name="frames",
    )(
        strip_movie,
        fitted,
        edge_a,
        edge_b,
        footprints,
        support,
        traces_rows,
        border_weight,
        coupling,
        turned,
        table,
        sides,
        row_filter,
        col_filter,
    )

    remainder = lax.all_to_all(leftover, "tile", split_axis=0, concat_axis=0, tiled=True)
    remainder = (
        remainder.reshape(tile_count, own_frames, tile_rows, columns)
        .transpose(1, 0, 2, 3)
        .reshape(own_frames, tile_count * tile_rows, columns)
    )
    all_traces = lax.all_gather(rounded, "frame", axis=0, tiled=True)
    trace_gram = lax.dot_general(
        all_traces, all_traces, (((0,), (0,)), ((), ())), preferred_element_type=jnp.float32
    )
    return (new_traces.T, trace_gram, remainder)


def solution(mesh):
    return jax.shard_map(
        per_device,
        mesh=mesh,
        in_specs=(
            P(("frame", "tile"), None, None),
            P("tile", None, None),
            P("tile", None),
            P("tile", "frame"),
            P("tile", None),
            P(),
        ),
        out_specs=(P("tile", "frame"), P("tile", None), P(("frame", "tile"), None, None)),
        check_vma=False,
    )
```

```python
import functools
import math

import jax
import jax.numpy as jnp
import numpy as np
from jax import lax
from jax.experimental import pallas as pl
from jax.experimental.pallas import tpu as pltpu
from jax.sharding import PartitionSpec as P

RR = 16
GR = 4
BR = 8
SWEEPS = 3
NR = 64
HALO = 24
LANES = 128
VMEM = pl.BlockSpec(memory_space=pltpu.VMEM)
ANY = pl.BlockSpec(memory_space=pl.ANY)


def split_high_low(values):
    high = values.astype(jnp.bfloat16)
    low = (values - high.astype(jnp.float32)).astype(jnp.bfloat16)
    return high, low


def filter_bands(tile_rows, columns):
    spots = np.arange(-GR, GR + 1).astype(np.float32)
    raw = np.exp(np.float32(-2.0) * spots * spots / np.float32(GR * GR)).astype(np.float32)
    taps = (raw / raw.sum(dtype=np.float32)).astype(np.float32)

    def band(count_out, count_in, shift):
        distance = np.arange(count_in)[None, :] - np.arange(count_out)[:, None] - shift
        inside = np.abs(distance) <= GR
        return np.where(inside, taps[np.clip(distance + GR, 0, 2 * GR)], np.float32(0.0))

    def parts(matrix):
        high = matrix.astype(jnp.bfloat16)
        low = (matrix - high.astype(np.float32)).astype(jnp.bfloat16)
        return high, low

    rows_high, rows_low = parts(band(tile_rows + 2 * RR, tile_rows + 2 * HALO, HALO - RR))
    cols_high, cols_low = parts(band(columns, columns, 0))
    return (
        jnp.asarray(np.concatenate([rows_high, rows_low], axis=1)),
        jnp.asarray(np.concatenate([cols_high, cols_high, cols_low], axis=0)),
    )


def border_tables(offsets, table_ref, sides_ref):
    columns = table_ref.shape[1]
    tile_rows = sides_ref.shape[0] // 2
    row = offsets[0:1, :]
    col = offsets[1:2, :]
    count = row.shape[1]
    along_top = row == -RR
    along_row = along_top | (row == RR)
    turned_lane = jnp.where(col > 0, columns - col, -col)
    kind = jnp.where(along_row, jnp.where(along_top, 0, 1), jnp.where(col < 0, 2, 3))
    lane = jnp.where(along_row, turned_lane, row + RR)
    kind_hot = jnp.where(kind == lax.broadcasted_iota(jnp.int32, (8, count), 0), 1.0, 0.0)
    lane_hot = jnp.where(lane == lax.broadcasted_iota(jnp.int32, (columns, count), 0), 1.0, 0.0)
    base = lax.dot_general(
        kind_hot.astype(jnp.bfloat16),
        lane_hot.astype(jnp.bfloat16),
        (((1,), (1,)), ((), ())),
        preferred_element_type=jnp.float32,
    )
    distance = lax.broadcasted_iota(jnp.int32, (columns, columns), 0) - lax.broadcasted_iota(
        jnp.int32, (columns, columns), 1
    )
    near = jnp.abs(distance) <= RR
    for kind_at in range(2):
        spread = jnp.broadcast_to(base[kind_at : kind_at + 1, :], (columns, columns))
        turned = pltpu.roll(spread, 0, 1, stride=1, stride_axis=0)
        table_ref[kind_at * columns : (kind_at + 1) * columns, :] = jnp.where(
            near, turned, 0.0
        ).astype(jnp.bfloat16)
    width = sides_ref.shape[1]
    for kind_at in range(2):
        spread = jnp.broadcast_to(base[2 + kind_at : 3 + kind_at, :width], (tile_rows, width))
        turned = pltpu.roll(spread, 0, 1, stride=1, stride_axis=0)
        sides_ref[kind_at * tile_rows : (kind_at + 1) * tile_rows, :] = turned.astype(
            jnp.bfloat16
        )


def kernel_pieces(tile_rows, movie_ref, pieces_ref):
    frames, image_rows, columns = movie_ref.shape
    count = image_rows // tile_rows
    for tile in range(count):
        for frame in range(frames):
            start = max(tile * tile_rows - HALO, 0)
            stop = min((tile + 1) * tile_rows + HALO, image_rows)
            rows = movie_ref[frame, start:stop, :]
            blank = jnp.zeros((tile_rows + 2 * HALO - (stop - start), columns), movie_ref.dtype)
            if tile == 0:
                rows = jnp.concatenate([blank, rows], axis=0)
            elif tile == count - 1:
                rows = jnp.concatenate([rows, blank], axis=0)
            pieces_ref[tile * frames + frame] = rows


def start_footprints(footprints_hbm, footprints_ref, arrived):
    copies = []
    for b in range(footprints_ref.shape[0] // BR):
        rows = pl.ds(b * BR, BR)
        copies.append(
            pltpu.make_async_copy(footprints_hbm.at[rows], footprints_ref.at[rows], arrived.at[b])
        )
        copies[-1].start()
    return copies


def kernel_components(
    footprints_hbm,
    support_hbm,
    traces_hbm,
    offsets_hbm,
    fitted_ref,
    edge_a_ref,
    edge_b_ref,
    coupling_ref,
    table_ref,
    sides_ref,
    footprints_ref,
    support_ref,
    traces_ref,
    offsets_ref,
    lined_ref,
    arrived,
    arrived_small,
):
    small = [
        pltpu.make_async_copy(source, target, arrived_small.at[i])
        for i, (source, target) in enumerate(
            [
                (offsets_hbm, offsets_ref),
                (support_hbm, support_ref),
                (traces_hbm, traces_ref),
            ]
        )
    ]
    for copy in small:
        copy.start()
    copies = start_footprints(footprints_hbm, footprints_ref, arrived)
    tile_rows, columns, components = footprints_ref.shape
    frames = traces_ref.shape[0]
    halves = columns // LANES
    block = BR * columns
    split = components // 256 * 256
    for copy in small:
        copy.wait()
    border_tables(offsets_ref[...], table_ref, sides_ref)
    traces = traces_ref[...]
    for b in range(tile_rows // BR):
        copies[b].wait()
        mask = support_ref[b : b + 1, :].astype(jnp.bfloat16)
        shaped = footprints_ref[b * BR : (b + 1) * BR].reshape(block, components) * mask
        turned = shaped.T
        fitted = jnp.dot(traces, turned, preferred_element_type=jnp.float32)
        for row in range(BR):
            for half in range(halves):
                start = row * columns + half * LANES
                lined_ref[half, pl.ds(b * BR + row, frames, stride=tile_rows), :] = fitted[
                    :, start : start + LANES
                ]
        left = jnp.dot(turned, shaped[:, :split], preferred_element_type=jnp.float32)
        right = jnp.dot(turned[split:], shaped[:, split:], preferred_element_type=jnp.float32)
        if b == 0:
            coupling_ref[:, :split] = left
            coupling_ref[split:, split:] = right
        else:
            coupling_ref[:, :split] += left
            coupling_ref[split:, split:] += right
    coupling_ref[:split, split:] = coupling_ref[split:, :split].T
    odd = lax.axis_index("tile") % 2 == 1
    for half in range(halves):
        lanes = slice(half * LANES, (half + 1) * LANES)
        for frame in range(frames):
            lines = lined_ref[half, frame * tile_rows : (frame + 1) * tile_rows, :]
            fitted_ref[frame, :, lanes] = lines
            top = lines[:HALO]
            bottom = lines[tile_rows - HALO :]
            edge_a_ref[frame, :, lanes] = jnp.where(odd, top, bottom).astype(jnp.bfloat16)
            edge_b_ref[frame, :, lanes] = jnp.where(odd, bottom, top).astype(jnp.bfloat16)


def kernel_frames(
    tile_count,
    movie_ref,
    fitted_ref,
    edge_a_ref,
    edge_b_ref,
    footprints_hbm,
    support_ref,
    traces_ref,
    weight_ref,
    coupling_ref,
    table_ref,
    sides_ref,
    row_filter_ref,
    col_filter_ref,
    new_traces_ref,
    rounded_ref,
    remainder_ref,
    cleaned_ref,
    refit_ref,
    footprints_ref,
    turned_ref,
    arrived,
):
    copies = start_footprints(footprints_hbm, footprints_ref, arrived)
    tile_rows, columns, components = footprints_ref.shape
    frames = traces_ref.shape[0]
    halves = columns // LANES
    span = tile_rows + 2 * RR
    tile = lax.axis_index("tile")
    odd = tile % 2 == 1

    row_number = tile * tile_rows - RR + lax.broadcasted_iota(jnp.int32, (span, 1), 0)
    inside = (row_number >= 0) & (row_number < tile_count * tile_rows)
    row_filter = jnp.where(inside, row_filter_ref[...].astype(jnp.float32), 0.0).astype(
        jnp.bfloat16
    )
    tall = []
    for frame in range(frames):
        edge_a = edge_a_ref[frame].astype(jnp.float32)
        edge_b = edge_b_ref[frame].astype(jnp.float32)
        fitted = jnp.concatenate(
            [
                jnp.where(odd, edge_a, edge_b),
                fitted_ref[frame],
                jnp.where(odd, edge_b, edge_a),
            ],
            axis=0,
        )
        first = (movie_ref[frame].astype(jnp.float32) - fitted).astype(jnp.bfloat16)
        tall.append(
            jnp.dot(
                row_filter,
                jnp.concatenate([first, first], axis=0),
                preferred_element_type=jnp.float32,
            )
        )
    high, low = split_high_low(jnp.concatenate(tall, axis=0))
    smooth = jnp.dot(
        jnp.concatenate([high, low, high], axis=1),
        col_filter_ref[...],
        preferred_element_type=jnp.float32,
    ).astype(jnp.bfloat16)
    sides = sides_ref[:, :span]
    lane = lax.broadcasted_iota(jnp.int32, (tile_rows, columns), 1)
    weight = weight_ref[...]
    for frame in range(frames):
        lines = smooth[frame * span : (frame + 1) * span]
        ends = jnp.concatenate([lines[:tile_rows], lines[2 * RR :]], axis=1)
        summed = jnp.dot(ends, table_ref[...], preferred_element_type=jnp.float32)
        mixed = jnp.dot(sides, lines, preferred_element_type=jnp.float32)
        west = pltpu.roll(mixed[:tile_rows], RR, 1)
        east = pltpu.roll(mixed[tile_rows:], columns - RR, 1)
        summed = summed + jnp.where(lane >= RR, west, 0.0)
        summed = summed + jnp.where(lane < columns - RR, east, 0.0)
        background = weight * summed * (1.0 / math.sqrt(NR))
        movie = movie_ref[frame, HALO : HALO + tile_rows, :].astype(jnp.float32)
        cleaned = (movie - background).astype(jnp.bfloat16).astype(jnp.float32)
        for half in range(halves):
            cleaned_ref[half, frame * tile_rows : (frame + 1) * tile_rows, :] = cleaned[
                :, half * LANES : (half + 1) * LANES
            ]

    block = BR * columns
    projected = jnp.zeros((frames, components), jnp.float32)
    for b in range(tile_rows // BR):
        copies[b].wait()
        mask = support_ref[b : b + 1, :]
        shaped = footprints_ref[b * BR : (b + 1) * BR].reshape(
            block, components
        ) * mask.astype(jnp.bfloat16)
        turned_ref[:, b * block : (b + 1) * block] = shaped.T
        part = jnp.zeros((frames, components), jnp.float32)
        for row in range(b * BR, (b + 1) * BR):
            pixels = jnp.concatenate(
                [
                    cleaned_ref[half, pl.ds(row, frames, stride=tile_rows), :]
                    for half in range(halves)
                ],
                axis=1,
            ).astype(jnp.bfloat16)
            part = part + jnp.dot(
                pixels, footprints_ref[row], preferred_element_type=jnp.float32
            )
        projected = projected + part * mask.astype(jnp.float32)

    coupling = coupling_ref[...]
    diagonal = lax.broadcasted_iota(jnp.int32, coupling.shape, 0) == lax.broadcasted_iota(
        jnp.int32, coupling.shape, 1
    )
    floor = jnp.maximum(
        jnp.sum(jnp.where(diagonal, coupling, 0.0), axis=0, keepdims=True), 1.0
    )
    coupling_high, coupling_low = split_high_low(coupling)
    state = traces_ref[...].astype(jnp.float32)
    for _ in range(SWEEPS):
        state_high, state_low = split_high_low(state)
        by_high = jnp.dot(
            jnp.concatenate([state_high, state_low], axis=0),
            coupling_high,
            preferred_element_type=jnp.float32,
        )
        by_low = jnp.dot(state_high, coupling_low, preferred_element_type=jnp.float32)
        moved = by_high[:frames] + (by_high[frames:] + by_low)
        state = jnp.maximum(state + (projected - moved) / floor, 0.0)
    rounded = state.astype(jnp.bfloat16)
    new_traces_ref[...] = state
    rounded_ref[...] = rounded

    for b in range(tile_rows // BR):
        refit = jnp.dot(
            rounded,
            turned_ref[:, b * block : (b + 1) * block],
            preferred_element_type=jnp.float32,
        )
        for row in range(BR):
            for half in range(halves):
                start = row * columns + half * LANES
                refit_ref[half, pl.ds(b * BR + row, frames, stride=tile_rows), :] = refit[
                    :, start : start + LANES
                ]
    for frame in range(frames):
        rows = slice(frame * tile_rows, (frame + 1) * tile_rows)
        for half in range(halves):
            remainder_ref[frame, :, half * LANES : (half + 1) * LANES] = (
                cleaned_ref[half, rows, :] - refit_ref[half, rows, :]
            ).astype(jnp.bfloat16)


def pairs(count, turn):
    if count & (count - 1):
        return [(i, (i + turn) % count) for i in range(count)]
    return [(i, i ^ turn) for i in range(count)]


def kernel_gram(*refs):
    traces = jnp.concatenate([ref[...] for ref in refs[:-1]], axis=0)
    refs[-1][...] = lax.dot_general(
        traces, traces, (((0,), (0,)), ((), ())), preferred_element_type=jnp.float32
    )


def per_device(movie, footprints, support, traces, border_weight, border_offsets):
    tile_count = lax.axis_size("tile")
    tile_rows, columns, components = footprints.shape
    own_frames = movie.shape[0]
    frames = own_frames * tile_count
    pixels = tile_rows * columns
    halves = columns // LANES
    extended = tile_rows + 2 * HALO
    lined = pltpu.VMEM((halves, frames * tile_rows, LANES), jnp.float32)

    pieces = pl.pallas_call(
        functools.partial(kernel_pieces, tile_rows),
        out_shape=jax.ShapeDtypeStruct((frames, extended, columns), movie.dtype),
        in_specs=[VMEM],
        out_specs=VMEM,
        name="pieces",
    )(movie)
    strip_movie = lax.all_to_all(pieces, "tile", split_axis=0, concat_axis=0, tiled=True)

    traces_rows = traces.T
    fitted, edge_a, edge_b, coupling, table, sides = pl.pallas_call(
        kernel_components,
        out_shape=[
            jax.ShapeDtypeStruct((frames, tile_rows, columns), jnp.float32),
            jax.ShapeDtypeStruct((frames, HALO, columns), jnp.bfloat16),
            jax.ShapeDtypeStruct((frames, HALO, columns), jnp.bfloat16),
            jax.ShapeDtypeStruct((components, components), jnp.float32),
            jax.ShapeDtypeStruct((2 * columns, columns), jnp.bfloat16),
            jax.ShapeDtypeStruct((2 * tile_rows, LANES), jnp.bfloat16),
        ],
        in_specs=[ANY] * 4,
        out_specs=[VMEM] * 6,
        scratch_shapes=[
            pltpu.VMEM(footprints.shape, footprints.dtype),
            pltpu.VMEM(support.shape, support.dtype),
            pltpu.VMEM(traces_rows.shape, traces.dtype),
            pltpu.VMEM(border_offsets.shape[::-1], border_offsets.dtype),
            lined,
            pltpu.SemaphoreType.DMA((tile_rows // BR,)),
            pltpu.SemaphoreType.DMA((3,)),
        ],
        compiler_params=pltpu.CompilerParams(vmem_limit_bytes=40 << 20),
        cost_estimate=pl.CostEstimate(
            flops=2 * pixels * components * components,
            bytes_accessed=4 * pixels * components,
            transcendentals=0,
        ),
        name="components",
    )(footprints, support, traces_rows, border_offsets.T)

    evens = [(i, i + 1) for i in range(0, tile_count - 1, 2)]
    odds = [(i, i + 1) for i in range(1, tile_count - 1, 2)]
    edge_a = lax.ppermute(edge_a, "tile", evens + [(j, i) for i, j in evens])
    edge_b = lax.ppermute(edge_b, "tile", odds + [(j, i) for i, j in odds])

    row_filter, col_filter = filter_bands(tile_rows, columns)
    new_traces, rounded, leftover = pl.pallas_call(
        functools.partial(kernel_frames, tile_count),
        out_shape=[
            jax.ShapeDtypeStruct((frames, components), jnp.float32),
            jax.ShapeDtypeStruct((frames, components), jnp.bfloat16),
            jax.ShapeDtypeStruct((frames, tile_rows, columns), jnp.bfloat16),
        ],
        in_specs=[VMEM] * 4 + [ANY] + [VMEM] * 8,
        out_specs=[VMEM] * 3,
        scratch_shapes=[
            lined,
            lined,
            pltpu.VMEM(footprints.shape, footprints.dtype),
            pltpu.VMEM((components, pixels), jnp.bfloat16),
            pltpu.SemaphoreType.DMA((tile_rows // BR,)),
        ],
        compiler_params=pltpu.CompilerParams(vmem_limit_bytes=48 << 20),
        cost_estimate=pl.CostEstimate(
            flops=8 * frames * pixels * components,
            bytes_accessed=4 * pixels * components,
            transcendentals=0,
        ),
        name="frames",
    )(
        strip_movie,
        fitted,
        edge_a,
        edge_b,
        footprints,
        support,
        traces_rows,
        border_weight,
        coupling,
        table,
        sides,
        row_filter,
        col_filter,
    )

    frame_count = lax.axis_size("frame")
    all_traces = [rounded] + [
        lax.ppermute(rounded, "frame", pairs(frame_count, turn)) for turn in range(1, frame_count)
    ]
    remainder = lax.all_to_all(leftover, "tile", split_axis=0, concat_axis=0, tiled=True)
    remainder = (
        remainder.reshape(tile_count, own_frames, tile_rows, columns)
        .transpose(1, 0, 2, 3)
        .reshape(own_frames, tile_count * tile_rows, columns)
    )
    trace_gram = pl.pallas_call(
        kernel_gram,
        out_shape=jax.ShapeDtypeStruct((components, components), jnp.float32),
        in_specs=[VMEM] * len(all_traces),
        out_specs=VMEM,
        name="gram",
    )(*all_traces)
    return (new_traces.T, trace_gram, remainder)


def solution(mesh):
    return jax.shard_map(
        per_device,
        mesh=mesh,
        in_specs=(
            P(("frame", "tile"), None, None),
            P("tile", None, None),
            P("tile", None),
            P("tile", "frame"),
            P("tile", None),
            P(),
        ),
        out_specs=(P("tile", "frame"), P("tile", None), P(("frame", "tile"), None, None)),
        check_vma=False,
    )
```

```python
import functools
import math

import jax
import jax.numpy as jnp
import numpy as np
from jax import lax
from jax.experimental import pallas as pl
from jax.experimental.pallas import tpu as pltpu
from jax.sharding import PartitionSpec as P

RR = 16
GR = 4
BR = 8
SWEEPS = 3
NR = 64
HALO = 24
LANES = 128
AHEAD = 3
VMEM = pl.BlockSpec(memory_space=pltpu.VMEM)
HBM = pl.BlockSpec(memory_space=pltpu.HBM)


def split_high_low(values):
    high = values.astype(jnp.bfloat16)
    low = (values - high.astype(jnp.float32)).astype(jnp.bfloat16)
    return high, low


def filter_bands(tile_rows, columns):
    spots = np.arange(-GR, GR + 1).astype(np.float32)
    raw = np.exp(np.float32(-2.0) * spots * spots / np.float32(GR * GR)).astype(np.float32)
    taps = (raw / raw.sum(dtype=np.float32)).astype(np.float32)

    def band(count_out, count_in, shift):
        distance = np.arange(count_in)[None, :] - np.arange(count_out)[:, None] - shift
        inside = np.abs(distance) <= GR
        return np.where(inside, taps[np.clip(distance + GR, 0, 2 * GR)], np.float32(0.0))

    def parts(matrix):
        high = matrix.astype(jnp.bfloat16)
        low = (matrix - high.astype(np.float32)).astype(jnp.bfloat16)
        return high, low

    rows_high, rows_low = parts(band(tile_rows + 2 * RR, tile_rows + 2 * HALO, HALO - RR))
    cols_high, cols_low = parts(band(columns, columns, 0))
    return (
        jnp.asarray(np.concatenate([rows_high, rows_low], axis=1)),
        jnp.asarray(np.concatenate([cols_high, cols_high, cols_low], axis=0)),
    )


def border_tables(offsets, table_ref, sides_ref):
    columns = table_ref.shape[1]
    tile_rows = sides_ref.shape[0] // 2
    row = offsets[0:1, :]
    col = offsets[1:2, :]
    count = row.shape[1]
    along_top = row == -RR
    along_row = along_top | (row == RR)
    turned_lane = jnp.where(col > 0, columns - col, -col)
    kind = jnp.where(along_row, jnp.where(along_top, 0, 1), jnp.where(col < 0, 2, 3))
    lane = jnp.where(along_row, turned_lane, row + RR)
    kind_hot = jnp.where(kind == lax.broadcasted_iota(jnp.int32, (8, count), 0), 1.0, 0.0)
    lane_hot = jnp.where(lane == lax.broadcasted_iota(jnp.int32, (columns, count), 0), 1.0, 0.0)
    base = lax.dot_general(
        kind_hot.astype(jnp.bfloat16),
        lane_hot.astype(jnp.bfloat16),
        (((1,), (1,)), ((), ())),
        preferred_element_type=jnp.float32,
    )
    distance = lax.broadcasted_iota(jnp.int32, (columns, columns), 0) - lax.broadcasted_iota(
        jnp.int32, (columns, columns), 1
    )
    near = jnp.abs(distance) <= RR
    for kind_at in range(2):
        spread = jnp.broadcast_to(base[kind_at : kind_at + 1, :], (columns, columns))
        turned = pltpu.roll(spread, 0, 1, stride=1, stride_axis=0)
        table_ref[kind_at * columns : (kind_at + 1) * columns, :] = jnp.where(
            near, turned, 0.0
        ).astype(jnp.bfloat16)
    width = sides_ref.shape[1]
    for kind_at in range(2):
        spread = jnp.broadcast_to(base[2 + kind_at : 3 + kind_at, :width], (tile_rows, width))
        turned = pltpu.roll(spread, 0, 1, stride=1, stride_axis=0)
        sides_ref[kind_at * tile_rows : (kind_at + 1) * tile_rows, :] = turned.astype(
            jnp.bfloat16
        )


class Footprints:
    def __init__(self, source, target, arrived):
        self.copies = []
        for b in range(target.shape[0] // BR):
            rows = pl.ds(b * BR, BR)
            self.copies.append(
                pltpu.make_async_copy(source.at[rows], target.at[rows], arrived.at[b])
            )
        for copy in self.copies[:AHEAD]:
            copy.start()

    def wait(self, b):
        self.copies[b].wait()
        if b + AHEAD < len(self.copies):
            self.copies[b + AHEAD].start()


def kernel_fitted(
    footprints_hbm,
    support_hbm,
    traces_hbm,
    offsets_hbm,
    fitted_ref,
    table_ref,
    sides_ref,
    footprints_ref,
    support_ref,
    traces_ref,
    offsets_ref,
    lined_ref,
    arrived,
    arrived_small,
):
    small = [
        pltpu.make_async_copy(source, target, arrived_small.at[i])
        for i, (source, target) in enumerate(
            [
                (offsets_hbm, offsets_ref),
                (support_hbm, support_ref),
                (traces_hbm, traces_ref),
            ]
        )
    ]
    for copy in small:
        copy.start()
    blocks = Footprints(footprints_hbm, footprints_ref, arrived)
    tile_rows, columns, components = footprints_ref.shape
    frames = traces_ref.shape[0]
    halves = columns // LANES
    block = BR * columns
    for copy in small:
        copy.wait()
    border_tables(offsets_ref[...], table_ref, sides_ref)
    traces = traces_ref[...]
    for b in range(tile_rows // BR):
        blocks.wait(b)
        fitted = lax.dot_general(
            traces * support_ref[b : b + 1, :].astype(jnp.bfloat16),
            footprints_ref[b * BR : (b + 1) * BR].reshape(block, components),
            (((1,), (1,)), ((), ())),
            preferred_element_type=jnp.float32,
        )
        for row in range(BR):
            for half in range(halves):
                start = row * columns + half * LANES
                lined_ref[half, pl.ds(b * BR + row, frames, stride=tile_rows), :] = fitted[
                    :, start : start + LANES
                ]
    for half in range(halves):
        for frame in range(frames):
            fitted_ref[frame, :, half * LANES : (half + 1) * LANES] = lined_ref[
                half, frame * tile_rows : (frame + 1) * tile_rows, :
            ]


def kernel_coupling(footprints_ref, support_ref, turned_ref, coupling_ref):
    tile_rows, columns, components = footprints_ref.shape
    block = BR * columns
    split = components // 256 * 256
    for b in range(tile_rows // BR):
        mask = support_ref[b : b + 1, :].astype(jnp.bfloat16)
        shaped = footprints_ref[b * BR : (b + 1) * BR].reshape(block, components) * mask
        turned = shaped.T
        turned_ref[:, b * block : (b + 1) * block] = turned
        left = jnp.dot(turned, shaped[:, :split], preferred_element_type=jnp.float32)
        right = jnp.dot(turned[split:], shaped[:, split:], preferred_element_type=jnp.float32)
        if b == 0:
            coupling_ref[:, :split] = left
            coupling_ref[split:, split:] = right
        else:
            coupling_ref[:, :split] += left
            coupling_ref[split:, split:] += right
    coupling_ref[:split, split:] = coupling_ref[split:, :split].T


def kernel_traces(
    tile_count,
    movie_ref,
    first_ref,
    edge_a_ref,
    edge_b_ref,
    footprints_ref,
    support_ref,
    traces_ref,
    weight_ref,
    coupling_ref,
    table_ref,
    sides_ref,
    row_filter_ref,
    col_filter_ref,
    new_traces_ref,
    rounded_ref,
    cleaned_ref,
):
    tile_rows, columns, components = footprints_ref.shape
    frames = traces_ref.shape[0]
    halves = columns // LANES
    span = tile_rows + 2 * RR
    tile = lax.axis_index("tile")
    odd = tile % 2 == 1

    row_number = tile * tile_rows - RR + lax.broadcasted_iota(jnp.int32, (span, 1), 0)
    inside = (row_number >= 0) & (row_number < tile_count * tile_rows)
    row_filter = jnp.where(inside, row_filter_ref[...].astype(jnp.float32), 0.0).astype(
        jnp.bfloat16
    )
    tall = []
    for frame in range(frames):
        edge_a = edge_a_ref[frame].astype(jnp.float32)
        edge_b = edge_b_ref[frame].astype(jnp.float32)
        first = jnp.concatenate(
            [
                jnp.where(odd, edge_a, edge_b),
                first_ref[frame].astype(jnp.float32),
                jnp.where(odd, edge_b, edge_a),
            ],
            axis=0,
        ).astype(jnp.bfloat16)
        tall.append(
            jnp.dot(
                row_filter,
                jnp.concatenate([first, first], axis=0),
                preferred_element_type=jnp.float32,
            )
        )
    high, low = split_high_low(jnp.concatenate(tall, axis=0))
    smooth = jnp.dot(
        jnp.concatenate([high, low, high], axis=1),
        col_filter_ref[...],
        preferred_element_type=jnp.float32,
    ).astype(jnp.bfloat16)
    sides = sides_ref[:, :span]
    lane = lax.broadcasted_iota(jnp.int32, (tile_rows, columns), 1)
    weight = weight_ref[...]
    for frame in range(frames):
        lines = smooth[frame * span : (frame + 1) * span]
        ends = jnp.concatenate([lines[:tile_rows], lines[2 * RR :]], axis=1)
        summed = jnp.dot(ends, table_ref[...], preferred_element_type=jnp.float32)
        mixed = jnp.dot(sides, lines, preferred_element_type=jnp.float32)
        west = pltpu.roll(mixed[:tile_rows], RR, 1)
        east = pltpu.roll(mixed[tile_rows:], columns - RR, 1)
        summed = summed + jnp.where(lane >= RR, west, 0.0)
        summed = summed + jnp.where(lane < columns - RR, east, 0.0)
        background = weight * summed * (1.0 / math.sqrt(NR))
        movie = movie_ref[frame].astype(jnp.float32)
        cleaned = (movie - background).astype(jnp.bfloat16).astype(jnp.float32)
        for half in range(halves):
            cleaned_ref[half, frame * tile_rows : (frame + 1) * tile_rows, :] = cleaned[
                :, half * LANES : (half + 1) * LANES
            ]

    projected = jnp.zeros((frames, components), jnp.float32)
    for b in range(tile_rows // BR):
        part = jnp.zeros((frames, components), jnp.float32)
        for row in range(b * BR, (b + 1) * BR):
            pixels = jnp.concatenate(
                [
                    cleaned_ref[half, pl.ds(row, frames, stride=tile_rows), :]
                    for half in range(halves)
                ],
                axis=1,
            ).astype(jnp.bfloat16)
            part = part + jnp.dot(
                pixels, footprints_ref[row], preferred_element_type=jnp.float32
            )
        projected = projected + part * support_ref[b : b + 1, :].astype(jnp.float32)

    coupling = coupling_ref[...]
    diagonal = lax.broadcasted_iota(jnp.int32, coupling.shape, 0) == lax.broadcasted_iota(
        jnp.int32, coupling.shape, 1
    )
    floor = jnp.maximum(
        jnp.sum(jnp.where(diagonal, coupling, 0.0), axis=0, keepdims=True), 1.0
    )
    coupling_high, coupling_low = split_high_low(coupling)
    state = traces_ref[...].astype(jnp.float32)
    for _ in range(SWEEPS):
        state_high, state_low = split_high_low(state)
        by_high = jnp.dot(
            jnp.concatenate([state_high, state_low], axis=0),
            coupling_high,
            preferred_element_type=jnp.float32,
        )
        by_low = jnp.dot(state_high, coupling_low, preferred_element_type=jnp.float32)
        moved = by_high[:frames] + (by_high[frames:] + by_low)
        state = jnp.maximum(state + (projected - moved) / floor, 0.0)
    rounded = state.astype(jnp.bfloat16)
    new_traces_ref[...] = state
    rounded_ref[...] = rounded


def kernel_refit(rounded_ref, turned_ref, cleaned_ref, remainder_ref, refit_ref):
    frames, tile_rows, columns = remainder_ref.shape
    halves = columns // LANES
    block = BR * columns
    rounded = rounded_ref[...]
    for b in range(tile_rows // BR):
        refit = jnp.dot(
            rounded,
            turned_ref[:, b * block : (b + 1) * block],
            preferred_element_type=jnp.float32,
        )
        for row in range(BR):
            for half in range(halves):
                start = row * columns + half * LANES
                refit_ref[half, pl.ds(b * BR + row, frames, stride=tile_rows), :] = refit[
                    :, start : start + LANES
                ]
    for frame in range(frames):
        rows = slice(frame * tile_rows, (frame + 1) * tile_rows)
        for half in range(halves):
            remainder_ref[frame, :, half * LANES : (half + 1) * LANES] = (
                cleaned_ref[half, rows, :] - refit_ref[half, rows, :]
            ).astype(jnp.bfloat16)


def pairs(count, turn):
    if count & (count - 1):
        return [(i, (i + turn) % count) for i in range(count)]
    return [(i, i ^ turn) for i in range(count)]


def kernel_gram(*refs):
    traces = jnp.concatenate([ref[...] for ref in refs[:-1]], axis=0)
    refs[-1][...] = lax.dot_general(
        traces, traces, (((0,), (0,)), ((), ())), preferred_element_type=jnp.float32
    )


def per_device(movie, footprints, support, traces, border_weight, border_offsets):
    tile_count = lax.axis_size("tile")
    tile_rows, columns, components = footprints.shape
    own_frames = movie.shape[0]
    frames = own_frames * tile_count
    pixels = tile_rows * columns
    halves = columns // LANES
    lined = pltpu.VMEM((halves, frames * tile_rows, LANES), jnp.float32)
    lined_shape = jax.ShapeDtypeStruct(lined.shape, lined.dtype)
    blocks = tile_rows // BR

    pieces = (
        movie.reshape(own_frames, tile_count, tile_rows, columns)
        .transpose(1, 0, 2, 3)
        .reshape(frames, tile_rows, columns)
    )
    strip_movie = lax.all_to_all(pieces, "tile", split_axis=0, concat_axis=0, tiled=True)

    traces_rows = traces.T
    pinned = [
        pltpu.with_memory_space_constraint(array, pltpu.HBM)
        for array in (footprints, support, traces_rows, border_offsets.T)
    ]
    fitted, table, sides = pl.pallas_call(
        kernel_fitted,
        out_shape=[
            jax.ShapeDtypeStruct((frames, tile_rows, columns), jnp.float32),
            jax.ShapeDtypeStruct((2 * columns, columns), jnp.bfloat16),
            jax.ShapeDtypeStruct((2 * tile_rows, LANES), jnp.bfloat16),
        ],
        in_specs=[HBM] * 4,
        out_specs=[VMEM] * 3,
        scratch_shapes=[
            pltpu.VMEM(footprints.shape, footprints.dtype),
            pltpu.VMEM(support.shape, support.dtype),
            pltpu.VMEM(traces_rows.shape, traces.dtype),
            pltpu.VMEM(border_offsets.shape[::-1], border_offsets.dtype),
            lined,
            pltpu.SemaphoreType.DMA((blocks,)),
            pltpu.SemaphoreType.DMA((3,)),
        ],
        compiler_params=pltpu.CompilerParams(vmem_limit_bytes=24 << 20),
        cost_estimate=pl.CostEstimate(
            flops=2 * frames * pixels * components,
            bytes_accessed=2 * pixels * components,
            transcendentals=0,
        ),
        name="fitted",
    )(*pinned)

    first = (strip_movie.astype(jnp.float32) - fitted).astype(jnp.bfloat16)
    odd = lax.axis_index("tile") % 2 == 1
    top = first[:, :HALO]
    bottom = first[:, tile_rows - HALO :]
    evens = [(i, i + 1) for i in range(0, tile_count - 1, 2)]
    odds = [(i, i + 1) for i in range(1, tile_count - 1, 2)]
    edge_a = lax.ppermute(
        jnp.where(odd, top, bottom), "tile", evens + [(j, i) for i, j in evens]
    )
    edge_b = lax.ppermute(
        jnp.where(odd, bottom, top), "tile", odds + [(j, i) for i, j in odds]
    )

    turned, coupling = pl.pallas_call(
        kernel_coupling,
        out_shape=[
            jax.ShapeDtypeStruct((components, pixels), jnp.bfloat16),
            jax.ShapeDtypeStruct((components, components), jnp.float32),
        ],
        in_specs=[VMEM] * 2,
        out_specs=[VMEM] * 2,
        compiler_params=pltpu.CompilerParams(vmem_limit_bytes=24 << 20),
        cost_estimate=pl.CostEstimate(
            flops=2 * pixels * components * components,
            bytes_accessed=4 * pixels * components,
            transcendentals=0,
        ),
        name="coupling",
    )(footprints, support)

    row_filter, col_filter = filter_bands(tile_rows, columns)
    new_traces, rounded, cleaned = pl.pallas_call(
        functools.partial(kernel_traces, tile_count),
        out_shape=[
            jax.ShapeDtypeStruct((frames, components), jnp.float32),
            jax.ShapeDtypeStruct((frames, components), jnp.bfloat16),
            lined_shape,
        ],
        in_specs=[VMEM] * 13,
        out_specs=[VMEM] * 3,
        compiler_params=pltpu.CompilerParams(vmem_limit_bytes=20 << 20),
        cost_estimate=pl.CostEstimate(
            flops=4 * frames * pixels * components,
            bytes_accessed=2 * pixels * components,
            transcendentals=0,
        ),
        name="traces",
    )(
        strip_movie,
        first,
        edge_a,
        edge_b,
        footprints,
        support,
        traces_rows,
        border_weight,
        coupling,
        table,
        sides,
        row_filter,
        col_filter,
    )
    leftover = pl.pallas_call(
        kernel_refit,
        out_shape=jax.ShapeDtypeStruct((frames, tile_rows, columns), jnp.bfloat16),
        in_specs=[VMEM] * 3,
        out_specs=VMEM,
        scratch_shapes=[lined],
        compiler_params=pltpu.CompilerParams(vmem_limit_bytes=20 << 20),
        cost_estimate=pl.CostEstimate(
            flops=2 * frames * pixels * components,
            bytes_accessed=2 * pixels * components,
            transcendentals=0,
        ),
        name="refit",
    )(rounded, turned, cleaned)

    frame_count = lax.axis_size("frame")
    all_traces = [rounded] + [
        lax.ppermute(rounded, "frame", pairs(frame_count, turn)) for turn in range(1, frame_count)
    ]
    remainder = lax.all_to_all(leftover, "tile", split_axis=0, concat_axis=0, tiled=True)
    remainder = (
        remainder.reshape(tile_count, own_frames, tile_rows, columns)
        .transpose(1, 0, 2, 3)
        .reshape(own_frames, tile_count * tile_rows, columns)
    )
    trace_gram = pl.pallas_call(
        kernel_gram,
        out_shape=jax.ShapeDtypeStruct((components, components), jnp.float32),
        in_specs=[VMEM] * len(all_traces),
        out_specs=VMEM,
        name="gram",
    )(*all_traces)
    return (new_traces.T, trace_gram, remainder)


def solution(mesh):
    return jax.shard_map(
        per_device,
        mesh=mesh,
        in_specs=(
            P(("frame", "tile"), None, None),
            P("tile", None, None),
            P("tile", None),
            P("tile", "frame"),
            P("tile", None),
            P(),
        ),
        out_specs=(P("tile", "frame"), P("tile", None), P(("frame", "tile"), None, None)),
        check_vma=False,
    )
```

```python
import functools
import math

import jax
import jax.numpy as jnp
import numpy as np
from jax import lax
from jax.experimental import pallas as pl
from jax.experimental.pallas import tpu as pltpu
from jax.sharding import PartitionSpec as P

RR = 16
GR = 4
BR = 8
SWEEPS = 3
NR = 64
HALO = 24
LANES = 128
AHEAD = 3
EARLY = 7
VMEM = pl.BlockSpec(memory_space=pltpu.VMEM)
HBM = pl.BlockSpec(memory_space=pltpu.HBM)


def split_high_low(values):
    high = values.astype(jnp.bfloat16)
    low = (values - high.astype(jnp.float32)).astype(jnp.bfloat16)
    return high, low


def filter_bands(tile_rows, columns):
    spots = np.arange(-GR, GR + 1).astype(np.float32)
    raw = np.exp(np.float32(-2.0) * spots * spots / np.float32(GR * GR)).astype(np.float32)
    taps = (raw / raw.sum(dtype=np.float32)).astype(np.float32)

    def band(count_out, count_in, shift):
        distance = np.arange(count_in)[None, :] - np.arange(count_out)[:, None] - shift
        inside = np.abs(distance) <= GR
        return np.where(inside, taps[np.clip(distance + GR, 0, 2 * GR)], np.float32(0.0))

    def parts(matrix):
        high = matrix.astype(jnp.bfloat16)
        low = (matrix - high.astype(np.float32)).astype(jnp.bfloat16)
        return high, low

    rows_high, rows_low = parts(band(tile_rows + 2 * RR, tile_rows + 2 * HALO, HALO - RR))
    cols_high, cols_low = parts(band(columns, columns, 0))
    return (
        jnp.asarray(np.concatenate([rows_high, rows_low], axis=1)),
        jnp.asarray(np.concatenate([cols_high, cols_high, cols_low], axis=0)),
    )


def border_tables(offsets, table_ref, sides_ref):
    columns = table_ref.shape[1]
    tile_rows = sides_ref.shape[0] // 2
    row = offsets[0:1, :]
    col = offsets[1:2, :]
    count = row.shape[1]
    along_top = row == -RR
    along_row = along_top | (row == RR)
    turned_lane = jnp.where(col > 0, columns - col, -col)
    kind = jnp.where(along_row, jnp.where(along_top, 0, 1), jnp.where(col < 0, 2, 3))
    lane = jnp.where(along_row, turned_lane, row + RR)
    kind_hot = jnp.where(kind == lax.broadcasted_iota(jnp.int32, (8, count), 0), 1.0, 0.0)
    lane_hot = jnp.where(lane == lax.broadcasted_iota(jnp.int32, (columns, count), 0), 1.0, 0.0)
    base = lax.dot_general(
        kind_hot.astype(jnp.bfloat16),
        lane_hot.astype(jnp.bfloat16),
        (((1,), (1,)), ((), ())),
        preferred_element_type=jnp.float32,
    )
    distance = lax.broadcasted_iota(jnp.int32, (columns, columns), 0) - lax.broadcasted_iota(
        jnp.int32, (columns, columns), 1
    )
    near = jnp.abs(distance) <= RR
    for kind_at in range(2):
        spread = jnp.broadcast_to(base[kind_at : kind_at + 1, :], (columns, columns))
        turned = pltpu.roll(spread, 0, 1, stride=1, stride_axis=0)
        table_ref[kind_at * columns : (kind_at + 1) * columns, :] = jnp.where(
            near, turned, 0.0
        ).astype(jnp.bfloat16)
    width = sides_ref.shape[1]
    for kind_at in range(2):
        spread = jnp.broadcast_to(base[2 + kind_at : 3 + kind_at, :width], (tile_rows, width))
        turned = pltpu.roll(spread, 0, 1, stride=1, stride_axis=0)
        sides_ref[kind_at * tile_rows : (kind_at + 1) * tile_rows, :] = turned.astype(
            jnp.bfloat16
        )


def block_copies(source, target, arrived, first=0):
    return [
        pltpu.make_async_copy(
            source.at[pl.ds((first + b) * BR, BR)], target.at[pl.ds(b * BR, BR)], arrived.at[b]
        )
        for b in range(target.shape[0] // BR)
    ]


def kernel_fitted(
    footprints_hbm,
    support_hbm,
    traces_hbm,
    fitted_ref,
    footprints_ref,
    support_ref,
    traces_ref,
    lined_ref,
    arrived,
    arrived_small,
):
    small = [
        pltpu.make_async_copy(source, target, arrived_small.at[i])
        for i, (source, target) in enumerate(
            [
                (support_hbm, support_ref),
                (traces_hbm, traces_ref),
            ]
        )
    ]
    for copy in small:
        copy.start()
    copies = block_copies(footprints_hbm, footprints_ref, arrived)
    for copy in copies[:AHEAD]:
        copy.start()
    tile_rows, columns, components = footprints_ref.shape
    frames = traces_ref.shape[0]
    halves = columns // LANES
    block = BR * columns
    for copy in small:
        copy.wait()
    traces = traces_ref[...]
    for b in range(tile_rows // BR):
        copies[b].wait()
        if b + AHEAD < len(copies):
            copies[b + AHEAD].start()
        fitted = lax.dot_general(
            traces * support_ref[b : b + 1, :].astype(jnp.bfloat16),
            footprints_ref[b * BR : (b + 1) * BR].reshape(block, components),
            (((1,), (1,)), ((), ())),
            preferred_element_type=jnp.float32,
        )
        for row in range(BR):
            for half in range(halves):
                start = row * columns + half * LANES
                lined_ref[half, pl.ds(b * BR + row, frames, stride=tile_rows), :] = fitted[
                    :, start : start + LANES
                ]
    for half in range(halves):
        for frame in range(frames):
            fitted_ref[frame, :, half * LANES : (half + 1) * LANES] = lined_ref[
                half, frame * tile_rows : (frame + 1) * tile_rows, :
            ]


def kernel_early(footprints_hbm, offsets_ref, early_ref, table_ref, sides_ref, arrived):
    copies = block_copies(footprints_hbm, early_ref, arrived)
    for copy in copies:
        copy.start()
    border_tables(offsets_ref[...], table_ref, sides_ref)
    for copy in copies:
        copy.wait()


def kernel_background(
    tile_count,
    movie_ref,
    first_ref,
    edge_a_ref,
    edge_b_ref,
    footprints_hbm,
    weight_ref,
    table_ref,
    sides_ref,
    row_filter_ref,
    col_filter_ref,
    cleaned_ref,
    late_ref,
    arrived,
):
    tile_rows, columns, components = footprints_hbm.shape
    copies = block_copies(
        footprints_hbm, late_ref, arrived, (tile_rows - late_ref.shape[0]) // BR
    )
    for copy in copies:
        copy.start()
    frames = movie_ref.shape[0]
    halves = columns // LANES
    span = tile_rows + 2 * RR
    tile = lax.axis_index("tile")
    odd = tile % 2 == 1

    row_number = tile * tile_rows - RR + lax.broadcasted_iota(jnp.int32, (span, 1), 0)
    inside = (row_number >= 0) & (row_number < tile_count * tile_rows)
    row_filter = jnp.where(inside, row_filter_ref[...].astype(jnp.float32), 0.0).astype(
        jnp.bfloat16
    )
    tall = []
    for frame in range(frames):
        edge_a = edge_a_ref[frame].astype(jnp.float32)
        edge_b = edge_b_ref[frame].astype(jnp.float32)
        first = jnp.concatenate(
            [
                jnp.where(odd, edge_a, edge_b),
                first_ref[frame].astype(jnp.float32),
                jnp.where(odd, edge_b, edge_a),
            ],
            axis=0,
        ).astype(jnp.bfloat16)
        tall.append(
            jnp.dot(
                row_filter,
                jnp.concatenate([first, first], axis=0),
                preferred_element_type=jnp.float32,
            )
        )
    high, low = split_high_low(jnp.concatenate(tall, axis=0))
    smooth = jnp.dot(
        jnp.concatenate([high, low, high], axis=1),
        col_filter_ref[...],
        preferred_element_type=jnp.float32,
    ).astype(jnp.bfloat16)
    sides = sides_ref[:, :span]
    lane = lax.broadcasted_iota(jnp.int32, (tile_rows, columns), 1)
    weight = weight_ref[...]
    for frame in range(frames):
        lines = smooth[frame * span : (frame + 1) * span]
        ends = jnp.concatenate([lines[:tile_rows], lines[2 * RR :]], axis=1)
        summed = jnp.dot(ends, table_ref[...], preferred_element_type=jnp.float32)
        mixed = jnp.dot(sides, lines, preferred_element_type=jnp.float32)
        west = pltpu.roll(mixed[:tile_rows], RR, 1)
        east = pltpu.roll(mixed[tile_rows:], columns - RR, 1)
        summed = summed + jnp.where(lane >= RR, west, 0.0)
        summed = summed + jnp.where(lane < columns - RR, east, 0.0)
        background = weight * summed * (1.0 / math.sqrt(NR))
        movie = movie_ref[frame].astype(jnp.float32)
        cleaned = (movie - background).astype(jnp.bfloat16).astype(jnp.float32)
        for half in range(halves):
            cleaned_ref[half, frame * tile_rows : (frame + 1) * tile_rows, :] = cleaned[
                :, half * LANES : (half + 1) * LANES
            ]

    for copy in copies:
        copy.wait()


def kernel_coupling(
    frames,
    early_ref,
    late_ref,
    cleaned_ref,
    support_ref,
    stacked_ref,
    coupling_ref,
    projected_ref,
    left_ref,
    right_ref,
):
    columns, components = early_ref.shape[1:]
    early = early_ref.shape[0] // BR
    tile_rows = early_ref.shape[0] + late_ref.shape[0]
    halves = columns // LANES
    block = BR * columns
    split = components // 256 * 256
    spare = stacked_ref.shape[0] - components - frames
    for b in range(tile_rows // BR):
        if b < early:
            raw = early_ref[b * BR : (b + 1) * BR]
        else:
            raw = late_ref[(b - early) * BR : (b - early + 1) * BR]
        shaped = raw.reshape(block, components) * support_ref[b : b + 1, :].astype(jnp.bfloat16)
        pixels = slice(b * block, (b + 1) * block)
        stacked_ref[:components, pixels] = shaped.T
        cleaned = jnp.concatenate(
            [
                cleaned_ref[half, pl.ds(row, frames, stride=tile_rows), :]
                for row in range(b * BR, (b + 1) * BR)
                for half in range(halves)
            ],
            axis=1,
        )
        if spare:
            cleaned = jnp.concatenate([cleaned, jnp.zeros((spare, block), jnp.float32)], axis=0)
        stacked_ref[components:, pixels] = cleaned.astype(jnp.bfloat16)
        left = jnp.dot(
            stacked_ref[:, pixels], shaped[:, :split], preferred_element_type=jnp.float32
        )
        right = jnp.dot(
            stacked_ref[split:, pixels], shaped[:, split:], preferred_element_type=jnp.float32
        )
        if b == 0:
            left_ref[...] = left
            right_ref[...] = right
        else:
            left_ref[...] += left
            right_ref[...] += right
    coupling_ref[:, :split] = left_ref[:components]
    coupling_ref[split:, split:] = right_ref[: components - split]
    coupling_ref[:split, split:] = left_ref[split:components].T
    projected_ref[...] = jnp.concatenate(
        [
            left_ref[components : components + frames],
            right_ref[components - split : components - split + frames],
        ],
        axis=1,
    )


def kernel_traces(
    stacked_ref,
    coupling_ref,
    projected_ref,
    traces_ref,
    cleaned_ref,
    new_traces_ref,
    rounded_ref,
    remainder_ref,
    refit_ref,
):
    frames, tile_rows, columns = remainder_ref.shape
    components = coupling_ref.shape[0]
    halves = columns // LANES
    block = BR * columns
    projected = projected_ref[...]
    coupling = coupling_ref[...]
    diagonal = lax.broadcasted_iota(jnp.int32, coupling.shape, 0) == lax.broadcasted_iota(
        jnp.int32, coupling.shape, 1
    )
    floor = jnp.maximum(
        jnp.sum(jnp.where(diagonal, coupling, 0.0), axis=0, keepdims=True), 1.0
    )
    coupling_high, coupling_low = split_high_low(coupling)
    state = traces_ref[...].astype(jnp.float32)
    for _ in range(SWEEPS):
        state_high, state_low = split_high_low(state)
        by_high = jnp.dot(
            jnp.concatenate([state_high, state_low], axis=0),
            coupling_high,
            preferred_element_type=jnp.float32,
        )
        by_low = jnp.dot(state_high, coupling_low, preferred_element_type=jnp.float32)
        moved = by_high[:frames] + (by_high[frames:] + by_low)
        state = jnp.maximum(state + (projected - moved) / floor, 0.0)
    rounded = state.astype(jnp.bfloat16)
    new_traces_ref[...] = state
    rounded_ref[...] = rounded

    for b in range(tile_rows // BR):
        refit = jnp.dot(
            rounded,
            stacked_ref[:components, b * block : (b + 1) * block],
            preferred_element_type=jnp.float32,
        )
        for row in range(BR):
            for half in range(halves):
                start = row * columns + half * LANES
                refit_ref[half, pl.ds(b * BR + row, frames, stride=tile_rows), :] = refit[
                    :, start : start + LANES
                ]
    for frame in range(frames):
        rows = slice(frame * tile_rows, (frame + 1) * tile_rows)
        for half in range(halves):
            remainder_ref[frame, :, half * LANES : (half + 1) * LANES] = (
                cleaned_ref[half, rows, :] - refit_ref[half, rows, :]
            ).astype(jnp.bfloat16)


def pairs(count, turn):
    if count & (count - 1):
        return [(i, (i + turn) % count) for i in range(count)]
    return [(i, i ^ turn) for i in range(count)]


def kernel_gram(*refs):
    traces = jnp.concatenate([ref[...] for ref in refs[:-1]], axis=0)
    refs[-1][...] = lax.dot_general(
        traces, traces, (((0,), (0,)), ((), ())), preferred_element_type=jnp.float32
    )


def per_device(movie, footprints, support, traces, border_weight, border_offsets):
    tile_count = lax.axis_size("tile")
    tile_rows, columns, components = footprints.shape
    own_frames = movie.shape[0]
    frames = own_frames * tile_count
    pixels = tile_rows * columns
    halves = columns // LANES
    lined = pltpu.VMEM((halves, frames * tile_rows, LANES), jnp.float32)
    blocks = tile_rows // BR

    pieces = (
        movie.reshape(own_frames, tile_count, tile_rows, columns)
        .transpose(1, 0, 2, 3)
        .reshape(frames, tile_rows, columns)
    )
    strip_movie = lax.all_to_all(pieces, "tile", split_axis=0, concat_axis=0, tiled=True)

    traces_rows = traces.T
    pinned = [
        pltpu.with_memory_space_constraint(array, pltpu.HBM)
        for array in (footprints, support, traces_rows)
    ]
    fitted = pl.pallas_call(
        kernel_fitted,
        out_shape=jax.ShapeDtypeStruct((frames, tile_rows, columns), jnp.float32),
        in_specs=[HBM] * 3,
        out_specs=VMEM,
        scratch_shapes=[
            pltpu.VMEM(footprints.shape, footprints.dtype),
            pltpu.VMEM(support.shape, support.dtype),
            pltpu.VMEM(traces_rows.shape, traces.dtype),
            lined,
            pltpu.SemaphoreType.DMA((blocks,)),
            pltpu.SemaphoreType.DMA((2,)),
        ],
        compiler_params=pltpu.CompilerParams(vmem_limit_bytes=24 << 20),
        cost_estimate=pl.CostEstimate(
            flops=2 * frames * pixels * components,
            bytes_accessed=2 * pixels * components,
            transcendentals=0,
        ),
        name="fitted",
    )(*pinned)

    first = (strip_movie.astype(jnp.float32) - fitted).astype(jnp.bfloat16)
    odd = lax.axis_index("tile") % 2 == 1
    top = first[:, :HALO]
    bottom = first[:, tile_rows - HALO :]
    evens = [(i, i + 1) for i in range(0, tile_count - 1, 2)]
    odds = [(i, i + 1) for i in range(1, tile_count - 1, 2)]
    edge_a = lax.ppermute(
        jnp.where(odd, top, bottom), "tile", evens + [(j, i) for i, j in evens]
    )
    edge_b = lax.ppermute(
        jnp.where(odd, bottom, top), "tile", odds + [(j, i) for i, j in odds]
    )

    early = blocks * EARLY // 8
    early_footprints, table, sides = pl.pallas_call(
        kernel_early,
        out_shape=[
            jax.ShapeDtypeStruct((early * BR, columns, components), footprints.dtype),
            jax.ShapeDtypeStruct((2 * columns, columns), jnp.bfloat16),
            jax.ShapeDtypeStruct((2 * tile_rows, LANES), jnp.bfloat16),
        ],
        in_specs=[HBM, VMEM],
        out_specs=[VMEM] * 3,
        scratch_shapes=[pltpu.SemaphoreType.DMA((early,))],
        compiler_params=pltpu.CompilerParams(vmem_limit_bytes=24 << 20),
        cost_estimate=pl.CostEstimate(
            flops=0, bytes_accessed=4 * early * BR * columns * components, transcendentals=0
        ),
        name="early",
    )(pinned[0], border_offsets.T)

    row_filter, col_filter = filter_bands(tile_rows, columns)
    cleaned, late_footprints = pl.pallas_call(
        functools.partial(kernel_background, tile_count),
        out_shape=[
            jax.ShapeDtypeStruct(lined.shape, lined.dtype),
            jax.ShapeDtypeStruct((tile_rows - early * BR, columns, components), footprints.dtype),
        ],
        in_specs=[VMEM] * 4 + [HBM] + [VMEM] * 5,
        out_specs=[VMEM] * 2,
        scratch_shapes=[pltpu.SemaphoreType.DMA((blocks - early,))],
        compiler_params=pltpu.CompilerParams(vmem_limit_bytes=20 << 20),
        name="background",
    )(
        strip_movie,
        first,
        edge_a,
        edge_b,
        pinned[0],
        border_weight,
        table,
        sides,
        row_filter,
        col_filter,
    )
    split = components // 256 * 256
    height = -(-(components + frames) // 16) * 16
    stacked, coupling, projected = pl.pallas_call(
        functools.partial(kernel_coupling, frames),
        out_shape=[
            jax.ShapeDtypeStruct((height, pixels), jnp.bfloat16),
            jax.ShapeDtypeStruct((components, components), jnp.float32),
            jax.ShapeDtypeStruct((frames, components), jnp.float32),
        ],
        in_specs=[VMEM] * 4,
        out_specs=[VMEM] * 3,
        scratch_shapes=[
            pltpu.VMEM((height, split), jnp.float32),
            pltpu.VMEM((height - split, components - split), jnp.float32),
        ],
        compiler_params=pltpu.CompilerParams(vmem_limit_bytes=24 << 20),
        name="coupling",
    )(early_footprints, late_footprints, cleaned, support)
    new_traces, rounded, leftover = pl.pallas_call(
        kernel_traces,
        out_shape=[
            jax.ShapeDtypeStruct((frames, components), jnp.float32),
            jax.ShapeDtypeStruct((frames, components), jnp.bfloat16),
            jax.ShapeDtypeStruct((frames, tile_rows, columns), jnp.bfloat16),
        ],
        in_specs=[VMEM] * 5,
        out_specs=[VMEM] * 3,
        scratch_shapes=[lined],
        compiler_params=pltpu.CompilerParams(vmem_limit_bytes=20 << 20),
        name="traces",
    )(stacked, coupling, projected, traces_rows, cleaned)

    frame_count = lax.axis_size("frame")
    all_traces = [rounded] + [
        lax.ppermute(rounded, "frame", pairs(frame_count, turn)) for turn in range(1, frame_count)
    ]
    remainder = lax.all_to_all(leftover, "tile", split_axis=0, concat_axis=0, tiled=True)
    remainder = (
        remainder.reshape(tile_count, own_frames, tile_rows, columns)
        .transpose(1, 0, 2, 3)
        .reshape(own_frames, tile_count * tile_rows, columns)
    )
    trace_gram = pl.pallas_call(
        kernel_gram,
        out_shape=jax.ShapeDtypeStruct((components, components), jnp.float32),
        in_specs=[VMEM] * len(all_traces),
        out_specs=VMEM,
        name="gram",
    )(*all_traces)
    return (new_traces.T, trace_gram, remainder)


def solution(mesh):
    return jax.shard_map(
        per_device,
        mesh=mesh,
        in_specs=(
            P(("frame", "tile"), None, None),
            P("tile", None, None),
            P("tile", None),
            P("tile", "frame"),
            P("tile", None),
            P(),
        ),
        out_specs=(P("tile", "frame"), P("tile", None), P(("frame", "tile"), None, None)),
        check_vma=False,
    )
```

```python
import functools
import math

import jax
import jax.numpy as jnp
import numpy as np
from jax import lax
from jax.experimental import pallas as pl
from jax.experimental.pallas import tpu as pltpu
from jax.sharding import PartitionSpec as P

RR = 16
GR = 4
BR = 8
SWEEPS = 3
NR = 64
HALO = 24
LANES = 128
AHEAD = 3
LATE = 1
VMEM = pl.BlockSpec(memory_space=pltpu.VMEM)
HBM = pl.BlockSpec(memory_space=pltpu.HBM)


def split_high_low(values):
    high = values.astype(jnp.bfloat16)
    low = (values - high.astype(jnp.float32)).astype(jnp.bfloat16)
    return high, low


def filter_bands(tile_rows, columns):
    spots = np.arange(-GR, GR + 1).astype(np.float32)
    raw = np.exp(np.float32(-2.0) * spots * spots / np.float32(GR * GR)).astype(np.float32)
    taps = (raw / raw.sum(dtype=np.float32)).astype(np.float32)

    def band(count_out, count_in, shift):
        distance = np.arange(count_in)[None, :] - np.arange(count_out)[:, None] - shift
        inside = np.abs(distance) <= GR
        return np.where(inside, taps[np.clip(distance + GR, 0, 2 * GR)], np.float32(0.0))

    def parts(matrix):
        high = matrix.astype(jnp.bfloat16)
        low = (matrix - high.astype(np.float32)).astype(jnp.bfloat16)
        return high, low

    rows_high, rows_low = parts(band(tile_rows + 2 * RR, tile_rows + 2 * HALO, HALO - RR))
    cols_high, cols_low = parts(band(columns, columns, 0))
    return (
        jnp.asarray(np.concatenate([rows_high, rows_low], axis=1)),
        jnp.asarray(np.concatenate([cols_high, cols_high, cols_low], axis=0)),
    )


def border_tables(offsets, table_ref, sides_ref):
    columns = table_ref.shape[1]
    tile_rows = sides_ref.shape[0] // 2
    row = offsets[0:1, :]
    col = offsets[1:2, :]
    count = row.shape[1]
    along_top = row == -RR
    along_row = along_top | (row == RR)
    turned_lane = jnp.where(col > 0, columns - col, -col)
    kind = jnp.where(along_row, jnp.where(along_top, 0, 1), jnp.where(col < 0, 2, 3))
    lane = jnp.where(along_row, turned_lane, row + RR)
    kind_hot = jnp.where(kind == lax.broadcasted_iota(jnp.int32, (8, count), 0), 1.0, 0.0)
    lane_hot = jnp.where(lane == lax.broadcasted_iota(jnp.int32, (columns, count), 0), 1.0, 0.0)
    base = lax.dot_general(
        kind_hot.astype(jnp.bfloat16),
        lane_hot.astype(jnp.bfloat16),
        (((1,), (1,)), ((), ())),
        preferred_element_type=jnp.float32,
    )
    distance = lax.broadcasted_iota(jnp.int32, (columns, columns), 0) - lax.broadcasted_iota(
        jnp.int32, (columns, columns), 1
    )
    near = jnp.abs(distance) <= RR
    for kind_at in range(2):
        spread = jnp.broadcast_to(base[kind_at : kind_at + 1, :], (columns, columns))
        turned = pltpu.roll(spread, 0, 1, stride=1, stride_axis=0)
        table_ref[kind_at * columns : (kind_at + 1) * columns, :] = jnp.where(
            near, turned, 0.0
        ).astype(jnp.bfloat16)
    width = sides_ref.shape[1]
    for kind_at in range(2):
        spread = jnp.broadcast_to(base[2 + kind_at : 3 + kind_at, :width], (tile_rows, width))
        turned = pltpu.roll(spread, 0, 1, stride=1, stride_axis=0)
        sides_ref[kind_at * tile_rows : (kind_at + 1) * tile_rows, :] = turned.astype(
            jnp.bfloat16
        )


def block_copies(source, target, arrived, first=0):
    return [
        pltpu.make_async_copy(
            source.at[pl.ds((first + b) * BR, BR)], target.at[pl.ds(b * BR, BR)], arrived.at[b]
        )
        for b in range(target.shape[0] // BR)
    ]


def kernel_fitted(
    footprints_hbm,
    support_hbm,
    traces_hbm,
    fitted_ref,
    kept_ref,
    others_ref,
    support_ref,
    traces_ref,
    lined_ref,
    arrived,
    arrived_small,
):
    small = [
        pltpu.make_async_copy(source, target, arrived_small.at[i])
        for i, (source, target) in enumerate(
            [
                (support_hbm, support_ref),
                (traces_hbm, traces_ref),
            ]
        )
    ]
    for copy in small:
        copy.start()
    tile_rows, columns, components = footprints_hbm.shape
    others = others_ref.shape[0]
    copies = block_copies(footprints_hbm, others_ref, arrived)
    copies.append(
        pltpu.make_async_copy(
            footprints_hbm.at[pl.ds(others, BR)], kept_ref, arrived.at[len(copies)]
        )
    )
    for copy in copies[:AHEAD]:
        copy.start()
    frames = traces_ref.shape[0]
    halves = columns // LANES
    block = BR * columns
    for copy in small:
        copy.wait()
    traces = traces_ref[...]
    for b in range(tile_rows // BR):
        copies[b].wait()
        if b + AHEAD < len(copies):
            copies[b + AHEAD].start()
        raw = kept_ref[...] if b * BR == others else others_ref[b * BR : (b + 1) * BR]
        fitted = lax.dot_general(
            traces * support_ref[b : b + 1, :].astype(jnp.bfloat16),
            raw.reshape(block, components),
            (((1,), (1,)), ((), ())),
            preferred_element_type=jnp.float32,
        )
        for row in range(BR):
            for half in range(halves):
                start = row * columns + half * LANES
                lined_ref[half, pl.ds(b * BR + row, frames, stride=tile_rows), :] = fitted[
                    :, start : start + LANES
                ]
    for half in range(halves):
        for frame in range(frames):
            fitted_ref[frame, :, half * LANES : (half + 1) * LANES] = lined_ref[
                half, frame * tile_rows : (frame + 1) * tile_rows, :
            ]


def kernel_early(footprints_hbm, offsets_ref, early_ref, table_ref, sides_ref, arrived):
    copies = block_copies(footprints_hbm, early_ref, arrived)
    for copy in copies:
        copy.start()
    border_tables(offsets_ref[...], table_ref, sides_ref)
    for copy in copies:
        copy.wait()


def kernel_background(
    tile_count,
    movie_ref,
    first_ref,
    edge_a_ref,
    edge_b_ref,
    footprints_hbm,
    weight_ref,
    table_ref,
    sides_ref,
    row_filter_ref,
    col_filter_ref,
    cleaned_ref,
    late_ref,
    arrived,
):
    frames, tile_rows, columns = movie_ref.shape
    late = tile_rows // BR - 1 - late_ref.shape[0] // BR
    copies = block_copies(footprints_hbm, late_ref, arrived, late)
    for copy in copies:
        copy.start()
    halves = columns // LANES
    span = tile_rows + 2 * RR
    tile = lax.axis_index("tile")
    odd = tile % 2 == 1

    row_number = tile * tile_rows - RR + lax.broadcasted_iota(jnp.int32, (span, 1), 0)
    inside = (row_number >= 0) & (row_number < tile_count * tile_rows)
    row_filter = jnp.where(inside, row_filter_ref[...].astype(jnp.float32), 0.0).astype(
        jnp.bfloat16
    )
    tall = []
    for frame in range(frames):
        edge_a = edge_a_ref[frame].astype(jnp.float32)
        edge_b = edge_b_ref[frame].astype(jnp.float32)
        first = jnp.concatenate(
            [
                jnp.where(odd, edge_a, edge_b),
                first_ref[frame].astype(jnp.float32),
                jnp.where(odd, edge_b, edge_a),
            ],
            axis=0,
        ).astype(jnp.bfloat16)
        tall.append(
            jnp.dot(
                row_filter,
                jnp.concatenate([first, first], axis=0),
                preferred_element_type=jnp.float32,
            )
        )
    high, low = split_high_low(jnp.concatenate(tall, axis=0))
    smooth = jnp.dot(
        jnp.concatenate([high, low, high], axis=1),
        col_filter_ref[...],
        preferred_element_type=jnp.float32,
    ).astype(jnp.bfloat16)
    sides = sides_ref[:, :span]
    lane = lax.broadcasted_iota(jnp.int32, (tile_rows, columns), 1)
    weight = weight_ref[...]
    for frame in range(frames):
        lines = smooth[frame * span : (frame + 1) * span]
        ends = jnp.concatenate([lines[:tile_rows], lines[2 * RR :]], axis=1)
        summed = jnp.dot(ends, table_ref[...], preferred_element_type=jnp.float32)
        mixed = jnp.dot(sides, lines, preferred_element_type=jnp.float32)
        west = pltpu.roll(mixed[:tile_rows], RR, 1)
        east = pltpu.roll(mixed[tile_rows:], columns - RR, 1)
        summed = summed + jnp.where(lane >= RR, west, 0.0)
        summed = summed + jnp.where(lane < columns - RR, east, 0.0)
        background = weight * summed * (1.0 / math.sqrt(NR))
        movie = movie_ref[frame].astype(jnp.float32)
        cleaned = (movie - background).astype(jnp.bfloat16).astype(jnp.float32)
        for half in range(halves):
            cleaned_ref[half, frame * tile_rows : (frame + 1) * tile_rows, :] = cleaned[
                :, half * LANES : (half + 1) * LANES
            ]

    for copy in copies:
        copy.wait()


def kernel_coupling(
    frames,
    early_ref,
    late_ref,
    kept_ref,
    cleaned_ref,
    support_ref,
    stacked_ref,
    coupling_ref,
    projected_ref,
    left_ref,
    right_ref,
):
    columns, components = early_ref.shape[1:]
    parts = [(part, b) for part in (early_ref, late_ref, kept_ref) for b in range(part.shape[0] // BR)]
    tile_rows = len(parts) * BR
    halves = columns // LANES
    block = BR * columns
    split = components // 256 * 256
    spare = stacked_ref.shape[0] - components - frames
    for b in range(tile_rows // BR):
        part, at = parts[b]
        raw = part[at * BR : (at + 1) * BR]
        shaped = raw.reshape(block, components) * support_ref[b : b + 1, :].astype(jnp.bfloat16)
        pixels = slice(b * block, (b + 1) * block)
        stacked_ref[:components, pixels] = shaped.T
        cleaned = jnp.concatenate(
            [
                cleaned_ref[half, pl.ds(row, frames, stride=tile_rows), :]
                for row in range(b * BR, (b + 1) * BR)
                for half in range(halves)
            ],
            axis=1,
        )
        if spare:
            cleaned = jnp.concatenate([cleaned, jnp.zeros((spare, block), jnp.float32)], axis=0)
        stacked_ref[components:, pixels] = cleaned.astype(jnp.bfloat16)
        left = jnp.dot(
            stacked_ref[:, pixels], shaped[:, :split], preferred_element_type=jnp.float32
        )
        right = jnp.dot(
            stacked_ref[split:, pixels], shaped[:, split:], preferred_element_type=jnp.float32
        )
        if b == 0:
            left_ref[...] = left
            right_ref[...] = right
        else:
            left_ref[...] += left
            right_ref[...] += right
    coupling_ref[:, :split] = left_ref[:components]
    coupling_ref[split:, split:] = right_ref[: components - split]
    coupling_ref[:split, split:] = left_ref[split:components].T
    projected_ref[...] = jnp.concatenate(
        [
            left_ref[components : components + frames],
            right_ref[components - split : components - split + frames],
        ],
        axis=1,
    )


def kernel_traces(
    stacked_ref,
    coupling_ref,
    projected_ref,
    traces_ref,
    cleaned_ref,
    new_traces_ref,
    rounded_ref,
    remainder_ref,
    refit_ref,
):
    frames, tile_rows, columns = remainder_ref.shape
    components = coupling_ref.shape[0]
    halves = columns // LANES
    block = BR * columns
    projected = projected_ref[...]
    coupling = coupling_ref[...]
    diagonal = lax.broadcasted_iota(jnp.int32, coupling.shape, 0) == lax.broadcasted_iota(
        jnp.int32, coupling.shape, 1
    )
    floor = jnp.maximum(
        jnp.sum(jnp.where(diagonal, coupling, 0.0), axis=0, keepdims=True), 1.0
    )
    coupling_high, coupling_low = split_high_low(coupling)
    state = traces_ref[...].astype(jnp.float32)
    for _ in range(SWEEPS):
        state_high, state_low = split_high_low(state)
        by_high = jnp.dot(
            jnp.concatenate([state_high, state_low], axis=0),
            coupling_high,
            preferred_element_type=jnp.float32,
        )
        by_low = jnp.dot(state_high, coupling_low, preferred_element_type=jnp.float32)
        moved = by_high[:frames] + (by_high[frames:] + by_low)
        state = jnp.maximum(state + (projected - moved) / floor, 0.0)
    rounded = state.astype(jnp.bfloat16)
    new_traces_ref[...] = state
    rounded_ref[...] = rounded

    for b in range(tile_rows // BR):
        refit = jnp.dot(
            rounded,
            stacked_ref[:components, b * block : (b + 1) * block],
            preferred_element_type=jnp.float32,
        )
        for row in range(BR):
            for half in range(halves):
                start = row * columns + half * LANES
                refit_ref[half, pl.ds(b * BR + row, frames, stride=tile_rows), :] = refit[
                    :, start : start + LANES
                ]
    for frame in range(frames):
        rows = slice(frame * tile_rows, (frame + 1) * tile_rows)
        for half in range(halves):
            remainder_ref[frame, :, half * LANES : (half + 1) * LANES] = (
                cleaned_ref[half, rows, :] - refit_ref[half, rows, :]
            ).astype(jnp.bfloat16)


def pairs(count, turn):
    if count & (count - 1):
        return [(i, (i + turn) % count) for i in range(count)]
    return [(i, i ^ turn) for i in range(count)]


def kernel_gram(*refs):
    traces = jnp.concatenate([ref[...] for ref in refs[:-1]], axis=0)
    refs[-1][...] = lax.dot_general(
        traces, traces, (((0,), (0,)), ((), ())), preferred_element_type=jnp.float32
    )


def per_device(movie, footprints, support, traces, border_weight, border_offsets):
    tile_count = lax.axis_size("tile")
    tile_rows, columns, components = footprints.shape
    own_frames = movie.shape[0]
    frames = own_frames * tile_count
    pixels = tile_rows * columns
    halves = columns // LANES
    lined = pltpu.VMEM((halves, frames * tile_rows, LANES), jnp.float32)
    blocks = tile_rows // BR

    pieces = (
        movie.reshape(own_frames, tile_count, tile_rows, columns)
        .transpose(1, 0, 2, 3)
        .reshape(frames, tile_rows, columns)
    )
    strip_movie = lax.all_to_all(pieces, "tile", split_axis=0, concat_axis=0, tiled=True)

    traces_rows = traces.T
    pinned = [
        pltpu.with_memory_space_constraint(array, pltpu.HBM)
        for array in (footprints, support, traces_rows)
    ]
    fitted, kept_footprints = pl.pallas_call(
        kernel_fitted,
        out_shape=[
            jax.ShapeDtypeStruct((frames, tile_rows, columns), jnp.float32),
            jax.ShapeDtypeStruct((BR, columns, components), footprints.dtype),
        ],
        in_specs=[HBM] * 3,
        out_specs=[VMEM] * 2,
        scratch_shapes=[
            pltpu.VMEM((tile_rows - BR, columns, components), footprints.dtype),
            pltpu.VMEM(support.shape, support.dtype),
            pltpu.VMEM(traces_rows.shape, traces.dtype),
            lined,
            pltpu.SemaphoreType.DMA((blocks,)),
            pltpu.SemaphoreType.DMA((2,)),
        ],
        compiler_params=pltpu.CompilerParams(vmem_limit_bytes=24 << 20),
        cost_estimate=pl.CostEstimate(
            flops=2 * frames * pixels * components,
            bytes_accessed=2 * pixels * components,
            transcendentals=0,
        ),
        name="fitted",
    )(*pinned)

    first = (strip_movie.astype(jnp.float32) - fitted).astype(jnp.bfloat16)
    odd = lax.axis_index("tile") % 2 == 1
    top = first[:, :HALO]
    bottom = first[:, tile_rows - HALO :]
    evens = [(i, i + 1) for i in range(0, tile_count - 1, 2)]
    odds = [(i, i + 1) for i in range(1, tile_count - 1, 2)]
    edge_a = lax.ppermute(
        jnp.where(odd, top, bottom), "tile", evens + [(j, i) for i, j in evens]
    )
    edge_b = lax.ppermute(
        jnp.where(odd, bottom, top), "tile", odds + [(j, i) for i, j in odds]
    )

    late_rows = BR * LATE
    early_rows = tile_rows - BR - late_rows
    early_footprints, table, sides = pl.pallas_call(
        kernel_early,
        out_shape=[
            jax.ShapeDtypeStruct((early_rows, columns, components), footprints.dtype),
            jax.ShapeDtypeStruct((2 * columns, columns), jnp.bfloat16),
            jax.ShapeDtypeStruct((2 * tile_rows, LANES), jnp.bfloat16),
        ],
        in_specs=[HBM, VMEM],
        out_specs=[VMEM] * 3,
        scratch_shapes=[pltpu.SemaphoreType.DMA((early_rows // BR,))],
        compiler_params=pltpu.CompilerParams(vmem_limit_bytes=24 << 20),
        cost_estimate=pl.CostEstimate(
            flops=0, bytes_accessed=4 * early_rows * columns * components, transcendentals=0
        ),
        name="early",
    )(pinned[0], border_offsets.T)

    row_filter, col_filter = filter_bands(tile_rows, columns)
    cleaned, late_footprints = pl.pallas_call(
        functools.partial(kernel_background, tile_count),
        out_shape=[
            jax.ShapeDtypeStruct(lined.shape, lined.dtype),
            jax.ShapeDtypeStruct((late_rows, columns, components), footprints.dtype),
        ],
        in_specs=[VMEM] * 4 + [HBM] + [VMEM] * 5,
        out_specs=[VMEM] * 2,
        scratch_shapes=[pltpu.SemaphoreType.DMA((LATE,))],
        compiler_params=pltpu.CompilerParams(vmem_limit_bytes=20 << 20),
        name="background",
    )(
        strip_movie,
        first,
        edge_a,
        edge_b,
        pinned[0],
        border_weight,
        table,
        sides,
        row_filter,
        col_filter,
    )
    split = components // 256 * 256
    height = -(-(components + frames) // 16) * 16
    stacked, coupling, projected = pl.pallas_call(
        functools.partial(kernel_coupling, frames),
        out_shape=[
            jax.ShapeDtypeStruct((height, pixels), jnp.bfloat16),
            jax.ShapeDtypeStruct((components, components), jnp.float32),
            jax.ShapeDtypeStruct((frames, components), jnp.float32),
        ],
        in_specs=[VMEM] * 5,
        out_specs=[VMEM] * 3,
        scratch_shapes=[
            pltpu.VMEM((height, split), jnp.float32),
            pltpu.VMEM((height - split, components - split), jnp.float32),
        ],
        compiler_params=pltpu.CompilerParams(vmem_limit_bytes=24 << 20),
        name="coupling",
    )(early_footprints, late_footprints, kept_footprints, cleaned, support)
    new_traces, rounded, leftover = pl.pallas_call(
        kernel_traces,
        out_shape=[
            jax.ShapeDtypeStruct((frames, components), jnp.float32),
            jax.ShapeDtypeStruct((frames, components), jnp.bfloat16),
            jax.ShapeDtypeStruct((frames, tile_rows, columns), jnp.bfloat16),
        ],
        in_specs=[VMEM] * 5,
        out_specs=[VMEM] * 3,
        scratch_shapes=[lined],
        compiler_params=pltpu.CompilerParams(vmem_limit_bytes=20 << 20),
        name="traces",
    )(stacked, coupling, projected, traces_rows, cleaned)

    frame_count = lax.axis_size("frame")
    all_traces = [rounded] + [
        lax.ppermute(rounded, "frame", pairs(frame_count, turn)) for turn in range(1, frame_count)
    ]
    remainder = lax.all_to_all(leftover, "tile", split_axis=0, concat_axis=0, tiled=True)
    remainder = (
        remainder.reshape(tile_count, own_frames, tile_rows, columns)
        .transpose(1, 0, 2, 3)
        .reshape(own_frames, tile_count * tile_rows, columns)
    )
    trace_gram = pl.pallas_call(
        kernel_gram,
        out_shape=jax.ShapeDtypeStruct((components, components), jnp.float32),
        in_specs=[VMEM] * len(all_traces),
        out_specs=VMEM,
        name="gram",
    )(*all_traces)
    return (new_traces.T, trace_gram, remainder)


def solution(mesh):
    return jax.shard_map(
        per_device,
        mesh=mesh,
        in_specs=(
            P(("frame", "tile"), None, None),
            P("tile", None, None),
            P("tile", None),
            P("tile", "frame"),
            P("tile", None),
            P(),
        ),
        out_specs=(P("tile", "frame"), P("tile", None), P(("frame", "tile"), None, None)),
        check_vma=False,
    )
```

```python
import functools
import math

import jax
import jax.numpy as jnp
import numpy as np
from jax import lax
from jax.experimental import pallas as pl
from jax.experimental.pallas import tpu as pltpu
from jax.sharding import PartitionSpec as P

RR = 16
GR = 4
BR = 8
SWEEPS = 3
NR = 64
HALO = 24
LANES = 128
AHEAD = 3
LATE = 1
VMEM = pl.BlockSpec(memory_space=pltpu.VMEM)
HBM = pl.BlockSpec(memory_space=pltpu.HBM)


def split_high_low(values):
    high = values.astype(jnp.bfloat16)
    low = (values - high.astype(jnp.float32)).astype(jnp.bfloat16)
    return high, low


def filter_bands(tile_rows, columns):
    spots = np.arange(-GR, GR + 1).astype(np.float32)
    raw = np.exp(np.float32(-2.0) * spots * spots / np.float32(GR * GR)).astype(np.float32)
    taps = (raw / raw.sum(dtype=np.float32)).astype(np.float32)

    def band(count_out, count_in, shift):
        distance = np.arange(count_in)[None, :] - np.arange(count_out)[:, None] - shift
        inside = np.abs(distance) <= GR
        return np.where(inside, taps[np.clip(distance + GR, 0, 2 * GR)], np.float32(0.0))

    def parts(matrix):
        high = matrix.astype(jnp.bfloat16)
        low = (matrix - high.astype(np.float32)).astype(jnp.bfloat16)
        return high, low

    rows_high, rows_low = parts(band(tile_rows + 2 * RR, tile_rows + 2 * HALO, HALO - RR))
    cols_high, cols_low = parts(band(columns, columns, 0))
    return (
        jnp.asarray(np.concatenate([rows_high, rows_low], axis=1)),
        jnp.asarray(np.concatenate([cols_high, cols_high, cols_low], axis=0)),
    )


def border_tables(offsets, table_ref, sides_ref):
    columns = table_ref.shape[1]
    tile_rows = sides_ref.shape[0] // 2
    row = offsets[0:1, :]
    col = offsets[1:2, :]
    count = row.shape[1]
    along_top = row == -RR
    along_row = along_top | (row == RR)
    turned_lane = jnp.where(col > 0, columns - col, -col)
    kind = jnp.where(along_row, jnp.where(along_top, 0, 1), jnp.where(col < 0, 2, 3))
    lane = jnp.where(along_row, turned_lane, row + RR)
    kind_hot = jnp.where(kind == lax.broadcasted_iota(jnp.int32, (8, count), 0), 1.0, 0.0)
    lane_hot = jnp.where(lane == lax.broadcasted_iota(jnp.int32, (columns, count), 0), 1.0, 0.0)
    base = lax.dot_general(
        kind_hot.astype(jnp.bfloat16),
        lane_hot.astype(jnp.bfloat16),
        (((1,), (1,)), ((), ())),
        preferred_element_type=jnp.float32,
    )
    distance = lax.broadcasted_iota(jnp.int32, (columns, columns), 0) - lax.broadcasted_iota(
        jnp.int32, (columns, columns), 1
    )
    near = jnp.abs(distance) <= RR
    for kind_at in range(2):
        spread = jnp.broadcast_to(base[kind_at : kind_at + 1, :], (columns, columns))
        turned = pltpu.roll(spread, 0, 1, stride=1, stride_axis=0)
        table_ref[kind_at * columns : (kind_at + 1) * columns, :] = jnp.where(
            near, turned, 0.0
        ).astype(jnp.bfloat16)
    width = sides_ref.shape[1]
    for kind_at in range(2):
        spread = jnp.broadcast_to(base[2 + kind_at : 3 + kind_at, :width], (tile_rows, width))
        turned = pltpu.roll(spread, 0, 1, stride=1, stride_axis=0)
        sides_ref[kind_at * tile_rows : (kind_at + 1) * tile_rows, :] = turned.astype(
            jnp.bfloat16
        )


def block_copies(source, target, arrived, first=0):
    return [
        pltpu.make_async_copy(
            source.at[pl.ds((first + b) * BR, BR)], target.at[pl.ds(b * BR, BR)], arrived.at[b]
        )
        for b in range(target.shape[0] // BR)
    ]


def kernel_fitted(
    footprints_hbm,
    support_hbm,
    traces_hbm,
    fitted_ref,
    kept_ref,
    others_ref,
    support_ref,
    traces_ref,
    lined_ref,
    arrived,
    arrived_small,
):
    small = [
        pltpu.make_async_copy(source, target, arrived_small.at[i])
        for i, (source, target) in enumerate(
            [
                (support_hbm, support_ref),
                (traces_hbm, traces_ref),
            ]
        )
    ]
    for copy in small:
        copy.start()
    tile_rows, columns, components = footprints_hbm.shape
    others = others_ref.shape[0]
    copies = block_copies(footprints_hbm, others_ref, arrived)
    copies.append(
        pltpu.make_async_copy(
            footprints_hbm.at[pl.ds(others, BR)], kept_ref, arrived.at[len(copies)]
        )
    )
    for copy in copies[:AHEAD]:
        copy.start()
    frames = traces_ref.shape[0]
    halves = columns // LANES
    block = BR * columns
    for copy in small:
        copy.wait()
    traces = traces_ref[...]
    for b in range(tile_rows // BR):
        copies[b].wait()
        if b + AHEAD < len(copies):
            copies[b + AHEAD].start()
        raw = kept_ref[...] if b * BR == others else others_ref[b * BR : (b + 1) * BR]
        fitted = lax.dot_general(
            traces * support_ref[b : b + 1, :].astype(jnp.bfloat16),
            raw.reshape(block, components),
            (((1,), (1,)), ((), ())),
            preferred_element_type=jnp.float32,
        )
        for row in range(BR):
            for half in range(halves):
                start = row * columns + half * LANES
                lined_ref[half, pl.ds(b * BR + row, frames, stride=tile_rows), :] = fitted[
                    :, start : start + LANES
                ]
    for half in range(halves):
        for frame in range(frames):
            fitted_ref[frame, :, half * LANES : (half + 1) * LANES] = lined_ref[
                half, frame * tile_rows : (frame + 1) * tile_rows, :
            ]


def kernel_early(footprints_hbm, offsets_ref, early_ref, table_ref, sides_ref, arrived):
    copies = block_copies(footprints_hbm, early_ref, arrived)
    for copy in copies:
        copy.start()
    border_tables(offsets_ref[...], table_ref, sides_ref)
    for copy in copies:
        copy.wait()


def kernel_background(
    tile_count,
    movie_ref,
    first_ref,
    edge_b_ref,
    edge_a_ref,
    footprints_hbm,
    weight_ref,
    table_ref,
    sides_ref,
    row_filter_ref,
    col_filter_ref,
    cleaned_ref,
    late_ref,
    arrived,
):
    frames, tile_rows, columns = movie_ref.shape
    late = tile_rows // BR - 1 - late_ref.shape[0] // BR
    copies = block_copies(footprints_hbm, late_ref, arrived, late)
    for copy in copies:
        copy.start()
    halves = columns // LANES
    span = tile_rows + 2 * RR
    tile = lax.axis_index("tile")
    odd = tile % 2 == 1

    row_number = tile * tile_rows - RR + lax.broadcasted_iota(jnp.int32, (span, 1), 0)
    inside = (row_number >= 0) & (row_number < tile_count * tile_rows)
    row_filter = jnp.where(inside, row_filter_ref[...].astype(jnp.float32), 0.0).astype(
        jnp.bfloat16
    )
    tall = []
    for frame in range(frames):
        edge_a = edge_a_ref[frame].astype(jnp.float32)
        edge_b = edge_b_ref[frame].astype(jnp.float32)
        first = jnp.concatenate(
            [
                jnp.where(odd, edge_a, edge_b),
                first_ref[frame].astype(jnp.float32),
                jnp.where(odd, edge_b, edge_a),
            ],
            axis=0,
        ).astype(jnp.bfloat16)
        tall.append(
            jnp.dot(
                row_filter,
                jnp.concatenate([first, first], axis=0),
                preferred_element_type=jnp.float32,
            )
        )
    high, low = split_high_low(jnp.concatenate(tall, axis=0))
    smooth = jnp.dot(
        jnp.concatenate([high, low, high], axis=1),
        col_filter_ref[...],
        preferred_element_type=jnp.float32,
    ).astype(jnp.bfloat16)
    sides = sides_ref[:, :span]
    lane = lax.broadcasted_iota(jnp.int32, (tile_rows, columns), 1)
    weight = weight_ref[...]
    for frame in range(frames):
        lines = smooth[frame * span : (frame + 1) * span]
        ends = jnp.concatenate([lines[:tile_rows], lines[2 * RR :]], axis=1)
        summed = jnp.dot(ends, table_ref[...], preferred_element_type=jnp.float32)
        mixed = jnp.dot(sides, lines, preferred_element_type=jnp.float32)
        west = pltpu.roll(mixed[:tile_rows], RR, 1)
        east = pltpu.roll(mixed[tile_rows:], columns - RR, 1)
        summed = summed + jnp.where(lane >= RR, west, 0.0)
        summed = summed + jnp.where(lane < columns - RR, east, 0.0)
        background = weight * summed * (1.0 / math.sqrt(NR))
        movie = movie_ref[frame].astype(jnp.float32)
        cleaned = (movie - background).astype(jnp.bfloat16).astype(jnp.float32)
        for half in range(halves):
            cleaned_ref[half, frame * tile_rows : (frame + 1) * tile_rows, :] = cleaned[
                :, half * LANES : (half + 1) * LANES
            ]

    for copy in copies:
        copy.wait()


def kernel_coupling(
    frames,
    early_ref,
    late_ref,
    kept_ref,
    cleaned_ref,
    support_ref,
    stacked_ref,
    coupling_ref,
    projected_ref,
    left_ref,
    right_ref,
):
    columns, components = early_ref.shape[1:]
    parts = [(part, b) for part in (early_ref, late_ref, kept_ref) for b in range(part.shape[0] // BR)]
    tile_rows = len(parts) * BR
    halves = columns // LANES
    block = BR * columns
    split = components // 256 * 256
    spare = stacked_ref.shape[0] - components - frames
    for b in range(tile_rows // BR):
        part, at = parts[b]
        raw = part[at * BR : (at + 1) * BR]
        shaped = raw.reshape(block, components) * support_ref[b : b + 1, :].astype(jnp.bfloat16)
        pixels = slice(b * block, (b + 1) * block)
        stacked_ref[:components, pixels] = shaped.T
        cleaned = jnp.concatenate(
            [
                cleaned_ref[half, pl.ds(row, frames, stride=tile_rows), :]
                for row in range(b * BR, (b + 1) * BR)
                for half in range(halves)
            ],
            axis=1,
        )
        if spare:
            cleaned = jnp.concatenate([cleaned, jnp.zeros((spare, block), jnp.float32)], axis=0)
        stacked_ref[components:, pixels] = cleaned.astype(jnp.bfloat16)
        left = jnp.dot(
            stacked_ref[:, pixels], shaped[:, :split], preferred_element_type=jnp.float32
        )
        right = jnp.dot(
            stacked_ref[split:, pixels], shaped[:, split:], preferred_element_type=jnp.float32
        )
        if b == 0:
            left_ref[...] = left
            right_ref[...] = right
        else:
            left_ref[...] += left
            right_ref[...] += right
    coupling_ref[:, :split] = left_ref[:components]
    coupling_ref[split:, split:] = right_ref[: components - split]
    coupling_ref[:split, split:] = left_ref[split:components].T
    projected_ref[...] = jnp.concatenate(
        [
            left_ref[components : components + frames],
            right_ref[components - split : components - split + frames],
        ],
        axis=1,
    )


def kernel_traces(
    stacked_ref,
    coupling_ref,
    projected_ref,
    traces_ref,
    cleaned_ref,
    new_traces_ref,
    rounded_ref,
    remainder_ref,
    refit_ref,
):
    frames, tile_rows, columns = remainder_ref.shape
    components = coupling_ref.shape[0]
    halves = columns // LANES
    block = BR * columns
    projected = projected_ref[...]
    coupling = coupling_ref[...]
    diagonal = lax.broadcasted_iota(jnp.int32, coupling.shape, 0) == lax.broadcasted_iota(
        jnp.int32, coupling.shape, 1
    )
    floor = jnp.maximum(
        jnp.sum(jnp.where(diagonal, coupling, 0.0), axis=0, keepdims=True), 1.0
    )
    coupling_high, coupling_low = split_high_low(coupling)
    state = traces_ref[...].astype(jnp.float32)
    for _ in range(SWEEPS):
        state_high, state_low = split_high_low(state)
        by_high = jnp.dot(
            jnp.concatenate([state_high, state_low], axis=0),
            coupling_high,
            preferred_element_type=jnp.float32,
        )
        by_low = jnp.dot(state_high, coupling_low, preferred_element_type=jnp.float32)
        moved = by_high[:frames] + (by_high[frames:] + by_low)
        state = jnp.maximum(state + (projected - moved) / floor, 0.0)
    rounded = state.astype(jnp.bfloat16)
    new_traces_ref[...] = state
    rounded_ref[...] = rounded

    for b in range(tile_rows // BR):
        refit = jnp.dot(
            rounded,
            stacked_ref[:components, b * block : (b + 1) * block],
            preferred_element_type=jnp.float32,
        )
        for row in range(BR):
            for half in range(halves):
                start = row * columns + half * LANES
                refit_ref[half, pl.ds(b * BR + row, frames, stride=tile_rows), :] = refit[
                    :, start : start + LANES
                ]
    for frame in range(frames):
        rows = slice(frame * tile_rows, (frame + 1) * tile_rows)
        for half in range(halves):
            remainder_ref[frame, :, half * LANES : (half + 1) * LANES] = (
                cleaned_ref[half, rows, :] - refit_ref[half, rows, :]
            ).astype(jnp.bfloat16)


def pairs(count, turn):
    if count & (count - 1):
        return [(i, (i + turn) % count) for i in range(count)]
    return [(i, i ^ turn) for i in range(count)]


def kernel_gram(*refs):
    traces = jnp.concatenate([ref[...] for ref in refs[:-1]], axis=0)
    refs[-1][...] = lax.dot_general(
        traces, traces, (((0,), (0,)), ((), ())), preferred_element_type=jnp.float32
    )


def per_device(movie, footprints, support, traces, border_weight, border_offsets):
    tile_count = lax.axis_size("tile")
    tile_rows, columns, components = footprints.shape
    own_frames = movie.shape[0]
    frames = own_frames * tile_count
    pixels = tile_rows * columns
    halves = columns // LANES
    lined = pltpu.VMEM((halves, frames * tile_rows, LANES), jnp.float32)
    blocks = tile_rows // BR

    pieces = (
        movie.reshape(own_frames, tile_count, tile_rows, columns)
        .transpose(1, 0, 2, 3)
        .reshape(frames, tile_rows, columns)
    )
    strip_movie = lax.all_to_all(pieces, "tile", split_axis=0, concat_axis=0, tiled=True)

    traces_rows = traces.T
    pinned = [
        pltpu.with_memory_space_constraint(array, pltpu.HBM)
        for array in (footprints, support, traces_rows)
    ]
    fitted, kept_footprints = pl.pallas_call(
        kernel_fitted,
        out_shape=[
            jax.ShapeDtypeStruct((frames, tile_rows, columns), jnp.float32),
            jax.ShapeDtypeStruct((BR, columns, components), footprints.dtype),
        ],
        in_specs=[HBM] * 3,
        out_specs=[VMEM] * 2,
        scratch_shapes=[
            pltpu.VMEM((tile_rows - BR, columns, components), footprints.dtype),
            pltpu.VMEM(support.shape, support.dtype),
            pltpu.VMEM(traces_rows.shape, traces.dtype),
            lined,
            pltpu.SemaphoreType.DMA((blocks,)),
            pltpu.SemaphoreType.DMA((2,)),
        ],
        compiler_params=pltpu.CompilerParams(vmem_limit_bytes=24 << 20),
        cost_estimate=pl.CostEstimate(
            flops=2 * frames * pixels * components,
            bytes_accessed=2 * pixels * components,
            transcendentals=0,
        ),
        name="fitted",
    )(*pinned)

    first = (strip_movie.astype(jnp.float32) - fitted).astype(jnp.bfloat16)
    odd = lax.axis_index("tile") % 2 == 1
    top = first[:, :HALO]
    bottom = first[:, tile_rows - HALO :]
    evens = [(i, i + 1) for i in range(0, tile_count - 1, 2)]
    odds = [(i, i + 1) for i in range(1, tile_count - 1, 2)]
    edge_b = lax.ppermute(
        jnp.where(odd, bottom, top), "tile", odds + [(j, i) for i, j in odds]
    )
    edge_a = lax.ppermute(
        jnp.where(odd, top, bottom), "tile", evens + [(j, i) for i, j in evens]
    )

    late_rows = BR * LATE
    early_rows = tile_rows - BR - late_rows
    early_footprints, table, sides = pl.pallas_call(
        kernel_early,
        out_shape=[
            jax.ShapeDtypeStruct((early_rows, columns, components), footprints.dtype),
            jax.ShapeDtypeStruct((2 * columns, columns), jnp.bfloat16),
            jax.ShapeDtypeStruct((2 * tile_rows, LANES), jnp.bfloat16),
        ],
        in_specs=[HBM, VMEM],
        out_specs=[VMEM] * 3,
        scratch_shapes=[pltpu.SemaphoreType.DMA((early_rows // BR,))],
        compiler_params=pltpu.CompilerParams(vmem_limit_bytes=24 << 20),
        cost_estimate=pl.CostEstimate(
            flops=0, bytes_accessed=4 * early_rows * columns * components, transcendentals=0
        ),
        name="early",
    )(pinned[0], border_offsets.T)

    row_filter, col_filter = filter_bands(tile_rows, columns)
    cleaned, late_footprints = pl.pallas_call(
        functools.partial(kernel_background, tile_count),
        out_shape=[
            jax.ShapeDtypeStruct(lined.shape, lined.dtype),
            jax.ShapeDtypeStruct((late_rows, columns, components), footprints.dtype),
        ],
        in_specs=[VMEM] * 4 + [HBM] + [VMEM] * 5,
        out_specs=[VMEM] * 2,
        scratch_shapes=[pltpu.SemaphoreType.DMA((LATE,))],
        compiler_params=pltpu.CompilerParams(vmem_limit_bytes=20 << 20),
        name="background",
    )(
        strip_movie,
        first,
        edge_b,
        edge_a,
        pinned[0],
        border_weight,
        table,
        sides,
        row_filter,
        col_filter,
    )
    split = components // 256 * 256
    height = -(-(components + frames) // 16) * 16
    stacked, coupling, projected = pl.pallas_call(
        functools.partial(kernel_coupling, frames),
        out_shape=[
            jax.ShapeDtypeStruct((height, pixels), jnp.bfloat16),
            jax.ShapeDtypeStruct((components, components), jnp.float32),
            jax.ShapeDtypeStruct((frames, components), jnp.float32),
        ],
        in_specs=[VMEM] * 5,
        out_specs=[VMEM] * 3,
        scratch_shapes=[
            pltpu.VMEM((height, split), jnp.float32),
            pltpu.VMEM((height - split, components - split), jnp.float32),
        ],
        compiler_params=pltpu.CompilerParams(vmem_limit_bytes=24 << 20),
        name="coupling",
    )(early_footprints, late_footprints, kept_footprints, cleaned, support)
    new_traces, rounded, leftover = pl.pallas_call(
        kernel_traces,
        out_shape=[
            jax.ShapeDtypeStruct((frames, components), jnp.float32),
            jax.ShapeDtypeStruct((frames, components), jnp.bfloat16),
            jax.ShapeDtypeStruct((frames, tile_rows, columns), jnp.bfloat16),
        ],
        in_specs=[VMEM] * 5,
        out_specs=[VMEM] * 3,
        scratch_shapes=[lined],
        compiler_params=pltpu.CompilerParams(vmem_limit_bytes=20 << 20),
        name="traces",
    )(stacked, coupling, projected, traces_rows, cleaned)

    frame_count = lax.axis_size("frame")
    all_traces = [rounded] + [
        lax.ppermute(rounded, "frame", pairs(frame_count, turn)) for turn in range(1, frame_count)
    ]
    remainder = lax.all_to_all(leftover, "tile", split_axis=0, concat_axis=0, tiled=True)
    remainder = (
        remainder.reshape(tile_count, own_frames, tile_rows, columns)
        .transpose(1, 0, 2, 3)
        .reshape(own_frames, tile_count * tile_rows, columns)
    )
    trace_gram = pl.pallas_call(
        kernel_gram,
        out_shape=jax.ShapeDtypeStruct((components, components), jnp.float32),
        in_specs=[VMEM] * len(all_traces),
        out_specs=VMEM,
        name="gram",
    )(*all_traces)
    return (new_traces.T, trace_gram, remainder)


def solution(mesh):
    return jax.shard_map(
        per_device,
        mesh=mesh,
        in_specs=(
            P(("frame", "tile"), None, None),
            P("tile", None, None),
            P("tile", None),
            P("tile", "frame"),
            P("tile", None),
            P(),
        ),
        out_specs=(P("tile", "frame"), P("tile", None), P(("frame", "tile"), None, None)),
        check_vma=False,
    )
```

```python
import functools
import math

import jax
import jax.numpy as jnp
import numpy as np
from jax import lax
from jax.experimental import pallas as pl
from jax.experimental.pallas import tpu as pltpu
from jax.sharding import PartitionSpec as P

RR = 16
GR = 4
BR = 8
SWEEPS = 3
NR = 64
HALO = 24
LANES = 128
AHEAD = 3
LATE = 1
VMEM = pl.BlockSpec(memory_space=pltpu.VMEM)
HBM = pl.BlockSpec(memory_space=pltpu.HBM)


def split_high_low(values):
    high = values.astype(jnp.bfloat16)
    low = (values - high.astype(jnp.float32)).astype(jnp.bfloat16)
    return high, low


def filter_bands(tile_rows, columns):
    spots = np.arange(-GR, GR + 1).astype(np.float32)
    raw = np.exp(np.float32(-2.0) * spots * spots / np.float32(GR * GR)).astype(np.float32)
    taps = (raw / raw.sum(dtype=np.float32)).astype(np.float32)

    def band(count_out, count_in, shift):
        distance = np.arange(count_in)[None, :] - np.arange(count_out)[:, None] - shift
        inside = np.abs(distance) <= GR
        return np.where(inside, taps[np.clip(distance + GR, 0, 2 * GR)], np.float32(0.0))

    def parts(matrix):
        high = matrix.astype(jnp.bfloat16)
        low = (matrix - high.astype(np.float32)).astype(jnp.bfloat16)
        return high, low

    rows_high, rows_low = parts(band(tile_rows + 2 * RR, tile_rows + 2 * HALO, HALO - RR))
    cols_high, cols_low = parts(band(columns, columns, 0))
    return (
        jnp.asarray(np.concatenate([rows_high, rows_low], axis=1)),
        jnp.asarray(np.concatenate([cols_high, cols_low], axis=0)),
    )


def border_tables(offsets, table_ref, sides_ref):
    columns = table_ref.shape[1]
    tile_rows = sides_ref.shape[0] // 2
    row = offsets[0:1, :]
    col = offsets[1:2, :]
    count = row.shape[1]
    along_top = row == -RR
    along_row = along_top | (row == RR)
    turned_lane = jnp.where(col > 0, columns - col, -col)
    kind = jnp.where(along_row, jnp.where(along_top, 0, 1), jnp.where(col < 0, 2, 3))
    lane = jnp.where(along_row, turned_lane, row + RR)
    kind_hot = jnp.where(kind == lax.broadcasted_iota(jnp.int32, (8, count), 0), 1.0, 0.0)
    lane_hot = jnp.where(lane == lax.broadcasted_iota(jnp.int32, (columns, count), 0), 1.0, 0.0)
    base = lax.dot_general(
        kind_hot.astype(jnp.bfloat16),
        lane_hot.astype(jnp.bfloat16),
        (((1,), (1,)), ((), ())),
        preferred_element_type=jnp.float32,
    )
    distance = lax.broadcasted_iota(jnp.int32, (columns, columns), 0) - lax.broadcasted_iota(
        jnp.int32, (columns, columns), 1
    )
    near = jnp.abs(distance) <= RR
    for kind_at in range(2):
        spread = jnp.broadcast_to(base[kind_at : kind_at + 1, :], (columns, columns))
        turned = pltpu.roll(spread, 0, 1, stride=1, stride_axis=0)
        table_ref[kind_at * columns : (kind_at + 1) * columns, :] = jnp.where(
            near, turned, 0.0
        ).astype(jnp.bfloat16)
    width = sides_ref.shape[1]
    for kind_at in range(2):
        spread = jnp.broadcast_to(base[2 + kind_at : 3 + kind_at, :width], (tile_rows, width))
        turned = pltpu.roll(spread, 0, 1, stride=1, stride_axis=0)
        sides_ref[kind_at * tile_rows : (kind_at + 1) * tile_rows, :] = turned.astype(
            jnp.bfloat16
        )


def block_copies(source, target, arrived, first=0):
    return [
        pltpu.make_async_copy(
            source.at[pl.ds((first + b) * BR, BR)], target.at[pl.ds(b * BR, BR)], arrived.at[b]
        )
        for b in range(target.shape[0] // BR)
    ]


def kernel_fitted(
    footprints_hbm,
    support_hbm,
    traces_hbm,
    fitted_ref,
    kept_ref,
    others_ref,
    support_ref,
    traces_ref,
    lined_ref,
    arrived,
    arrived_small,
):
    small = [
        pltpu.make_async_copy(source, target, arrived_small.at[i])
        for i, (source, target) in enumerate(
            [
                (support_hbm, support_ref),
                (traces_hbm, traces_ref),
            ]
        )
    ]
    for copy in small:
        copy.start()
    tile_rows, columns, components = footprints_hbm.shape
    others = others_ref.shape[0]
    copies = block_copies(footprints_hbm, others_ref, arrived)
    copies.append(
        pltpu.make_async_copy(
            footprints_hbm.at[pl.ds(others, BR)], kept_ref, arrived.at[len(copies)]
        )
    )
    for copy in copies[:AHEAD]:
        copy.start()
    frames = traces_ref.shape[0]
    halves = columns // LANES
    block = BR * columns
    for copy in small:
        copy.wait()
    traces = traces_ref[...]
    for b in range(tile_rows // BR):
        copies[b].wait()
        if b + AHEAD < len(copies):
            copies[b + AHEAD].start()
        raw = kept_ref[...] if b * BR == others else others_ref[b * BR : (b + 1) * BR]
        fitted = lax.dot_general(
            traces * support_ref[b : b + 1, :].astype(jnp.bfloat16),
            raw.reshape(block, components),
            (((1,), (1,)), ((), ())),
            preferred_element_type=jnp.float32,
        )
        for row in range(BR):
            for half in range(halves):
                start = row * columns + half * LANES
                lined_ref[half, pl.ds(b * BR + row, frames, stride=tile_rows), :] = fitted[
                    :, start : start + LANES
                ]
    for half in range(halves):
        for frame in range(frames):
            fitted_ref[frame, :, half * LANES : (half + 1) * LANES] = lined_ref[
                half, frame * tile_rows : (frame + 1) * tile_rows, :
            ]


def kernel_early(footprints_hbm, offsets_ref, early_ref, table_ref, sides_ref, arrived):
    copies = block_copies(footprints_hbm, early_ref, arrived)
    for copy in copies:
        copy.start()
    border_tables(offsets_ref[...], table_ref, sides_ref)
    for copy in copies:
        copy.wait()


def kernel_background(
    tile_count,
    movie_ref,
    first_ref,
    edge_b_ref,
    edge_a_ref,
    footprints_hbm,
    weight_ref,
    table_ref,
    sides_ref,
    row_filter_ref,
    col_filter_ref,
    cleaned_ref,
    late_ref,
    arrived,
):
    frames, tile_rows, columns = movie_ref.shape
    late = tile_rows // BR - 1 - late_ref.shape[0] // BR
    copies = block_copies(footprints_hbm, late_ref, arrived, late)
    for copy in copies:
        copy.start()
    halves = columns // LANES
    span = tile_rows + 2 * RR
    tile = lax.axis_index("tile")
    odd = tile % 2 == 1

    row_number = tile * tile_rows - RR + lax.broadcasted_iota(jnp.int32, (span, 1), 0)
    inside = (row_number >= 0) & (row_number < tile_count * tile_rows)
    row_filter = jnp.where(inside, row_filter_ref[...].astype(jnp.float32), 0.0).astype(
        jnp.bfloat16
    )
    tall = []
    for frame in range(frames):
        edge_a = edge_a_ref[frame].astype(jnp.float32)
        edge_b = edge_b_ref[frame].astype(jnp.float32)
        first = jnp.concatenate(
            [
                jnp.where(odd, edge_a, edge_b),
                first_ref[frame].astype(jnp.float32),
                jnp.where(odd, edge_b, edge_a),
            ],
            axis=0,
        ).astype(jnp.bfloat16)
        tall.append(
            jnp.dot(
                row_filter,
                jnp.concatenate([first, first], axis=0),
                preferred_element_type=jnp.float32,
            )
        )
    high = jnp.concatenate(tall, axis=0).astype(jnp.bfloat16)
    smooth = jnp.dot(
        jnp.concatenate([high, high], axis=1),
        col_filter_ref[...],
        preferred_element_type=jnp.float32,
    ).astype(jnp.bfloat16)
    sides = sides_ref[:, :span]
    lane = lax.broadcasted_iota(jnp.int32, (tile_rows, columns), 1)
    weight = weight_ref[...]
    for frame in range(frames):
        lines = smooth[frame * span : (frame + 1) * span]
        ends = jnp.concatenate([lines[:tile_rows], lines[2 * RR :]], axis=1)
        summed = jnp.dot(ends, table_ref[...], preferred_element_type=jnp.float32)
        mixed = jnp.dot(sides, lines, preferred_element_type=jnp.float32)
        west = pltpu.roll(mixed[:tile_rows], RR, 1)
        east = pltpu.roll(mixed[tile_rows:], columns - RR, 1)
        summed = summed + jnp.where(lane >= RR, west, 0.0)
        summed = summed + jnp.where(lane < columns - RR, east, 0.0)
        background = weight * summed * (1.0 / math.sqrt(NR))
        movie = movie_ref[frame].astype(jnp.float32)
        cleaned = (movie - background).astype(jnp.bfloat16).astype(jnp.float32)
        for half in range(halves):
            cleaned_ref[half, frame * tile_rows : (frame + 1) * tile_rows, :] = cleaned[
                :, half * LANES : (half + 1) * LANES
            ]

    for copy in copies:
        copy.wait()


def kernel_coupling(
    frames,
    early_ref,
    late_ref,
    kept_ref,
    cleaned_ref,
    support_ref,
    stacked_ref,
    coupling_ref,
    projected_ref,
    left_ref,
    right_ref,
):
    columns, components = early_ref.shape[1:]
    parts = [(part, b) for part in (early_ref, late_ref, kept_ref) for b in range(part.shape[0] // BR)]
    tile_rows = len(parts) * BR
    halves = columns // LANES
    block = BR * columns
    split = components // 256 * 256
    spare = stacked_ref.shape[0] - components - frames
    for b in range(tile_rows // BR):
        part, at = parts[b]
        raw = part[at * BR : (at + 1) * BR]
        shaped = raw.reshape(block, components) * support_ref[b : b + 1, :].astype(jnp.bfloat16)
        pixels = slice(b * block, (b + 1) * block)
        stacked_ref[:components, pixels] = shaped.T
        cleaned = jnp.concatenate(
            [
                cleaned_ref[half, pl.ds(row, frames, stride=tile_rows), :]
                for row in range(b * BR, (b + 1) * BR)
                for half in range(halves)
            ],
            axis=1,
        )
        if spare:
            cleaned = jnp.concatenate([cleaned, jnp.zeros((spare, block), jnp.float32)], axis=0)
        stacked_ref[components:, pixels] = cleaned.astype(jnp.bfloat16)
        left = jnp.dot(
            stacked_ref[:, pixels], shaped[:, :split], preferred_element_type=jnp.float32
        )
        right = jnp.dot(
            stacked_ref[split:, pixels], shaped[:, split:], preferred_element_type=jnp.float32
        )
        if b == 0:
            left_ref[...] = left
            right_ref[...] = right
        else:
            left_ref[...] += left
            right_ref[...] += right
    coupling_ref[:, :split] = left_ref[:components]
    coupling_ref[split:, split:] = right_ref[: components - split]
    coupling_ref[:split, split:] = left_ref[split:components].T
    projected_ref[...] = jnp.concatenate(
        [
            left_ref[components : components + frames],
            right_ref[components - split : components - split + frames],
        ],
        axis=1,
    )


def kernel_traces(
    stacked_ref,
    coupling_ref,
    projected_ref,
    traces_ref,
    cleaned_ref,
    new_traces_ref,
    rounded_ref,
    remainder_ref,
    refit_ref,
):
    frames, tile_rows, columns = remainder_ref.shape
    components = coupling_ref.shape[0]
    halves = columns // LANES
    block = BR * columns
    projected = projected_ref[...]
    coupling = coupling_ref[...]
    diagonal = lax.broadcasted_iota(jnp.int32, coupling.shape, 0) == lax.broadcasted_iota(
        jnp.int32, coupling.shape, 1
    )
    floor = jnp.maximum(
        jnp.sum(jnp.where(diagonal, coupling, 0.0), axis=0, keepdims=True), 1.0
    )
    coupling_high, coupling_low = split_high_low(coupling)
    state = traces_ref[...].astype(jnp.float32)
    for _ in range(SWEEPS):
        state_high, state_low = split_high_low(state)
        by_high = jnp.dot(
            jnp.concatenate([state_high, state_low], axis=0),
            coupling_high,
            preferred_element_type=jnp.float32,
        )
        by_low = jnp.dot(state_high, coupling_low, preferred_element_type=jnp.float32)
        moved = by_high[:frames] + (by_high[frames:] + by_low)
        state = jnp.maximum(state + (projected - moved) / floor, 0.0)
    rounded = state.astype(jnp.bfloat16)
    new_traces_ref[...] = state
    rounded_ref[...] = rounded

    for b in range(tile_rows // BR):
        refit = jnp.dot(
            rounded,
            stacked_ref[:components, b * block : (b + 1) * block],
            preferred_element_type=jnp.float32,
        )
        for row in range(BR):
            for half in range(halves):
                start = row * columns + half * LANES
                refit_ref[half, pl.ds(b * BR + row, frames, stride=tile_rows), :] = refit[
                    :, start : start + LANES
                ]
    for frame in range(frames):
        rows = slice(frame * tile_rows, (frame + 1) * tile_rows)
        for half in range(halves):
            remainder_ref[frame, :, half * LANES : (half + 1) * LANES] = (
                cleaned_ref[half, rows, :] - refit_ref[half, rows, :]
            ).astype(jnp.bfloat16)


def pairs(count, turn):
    if count & (count - 1):
        return [(i, (i + turn) % count) for i in range(count)]
    return [(i, i ^ turn) for i in range(count)]


def kernel_gram(*refs):
    traces = jnp.concatenate([ref[...] for ref in refs[:-1]], axis=0)
    refs[-1][...] = lax.dot_general(
        traces, traces, (((0,), (0,)), ((), ())), preferred_element_type=jnp.float32
    )


def per_device(movie, footprints, support, traces, border_weight, border_offsets):
    tile_count = lax.axis_size("tile")
    tile_rows, columns, components = footprints.shape
    own_frames = movie.shape[0]
    frames = own_frames * tile_count
    pixels = tile_rows * columns
    halves = columns // LANES
    lined = pltpu.VMEM((halves, frames * tile_rows, LANES), jnp.float32)
    blocks = tile_rows // BR

    pieces = (
        movie.reshape(own_frames, tile_count, tile_rows, columns)
        .transpose(1, 0, 2, 3)
        .reshape(frames, tile_rows, columns)
    )
    strip_movie = lax.all_to_all(pieces, "tile", split_axis=0, concat_axis=0, tiled=True)

    traces_rows = traces.T
    pinned = [
        pltpu.with_memory_space_constraint(array, pltpu.HBM)
        for array in (footprints, support, traces_rows)
    ]
    fitted, kept_footprints = pl.pallas_call(
        kernel_fitted,
        out_shape=[
            jax.ShapeDtypeStruct((frames, tile_rows, columns), jnp.float32),
            jax.ShapeDtypeStruct((BR, columns, components), footprints.dtype),
        ],
        in_specs=[HBM] * 3,
        out_specs=[VMEM] * 2,
        scratch_shapes=[
            pltpu.VMEM((tile_rows - BR, columns, components), footprints.dtype),
            pltpu.VMEM(support.shape, support.dtype),
            pltpu.VMEM(traces_rows.shape, traces.dtype),
            lined,
            pltpu.SemaphoreType.DMA((blocks,)),
            pltpu.SemaphoreType.DMA((2,)),
        ],
        compiler_params=pltpu.CompilerParams(vmem_limit_bytes=24 << 20),
        cost_estimate=pl.CostEstimate(
            flops=2 * frames * pixels * components,
            bytes_accessed=2 * pixels * components,
            transcendentals=0,
        ),
        name="fitted",
    )(*pinned)

    first = (strip_movie.astype(jnp.float32) - fitted).astype(jnp.bfloat16)
    odd = lax.axis_index("tile") % 2 == 1
    top = first[:, :HALO]
    bottom = first[:, tile_rows - HALO :]
    evens = [(i, i + 1) for i in range(0, tile_count - 1, 2)]
    odds = [(i, i + 1) for i in range(1, tile_count - 1, 2)]
    edge_b = lax.ppermute(
        jnp.where(odd, bottom, top), "tile", odds + [(j, i) for i, j in odds]
    )
    edge_a = lax.ppermute(
        jnp.where(odd, top, bottom), "tile", evens + [(j, i) for i, j in evens]
    )

    late_rows = BR * LATE
    early_rows = tile_rows - BR - late_rows
    early_footprints, table, sides = pl.pallas_call(
        kernel_early,
        out_shape=[
            jax.ShapeDtypeStruct((early_rows, columns, components), footprints.dtype),
            jax.ShapeDtypeStruct((2 * columns, columns), jnp.bfloat16),
            jax.ShapeDtypeStruct((2 * tile_rows, LANES), jnp.bfloat16),
        ],
        in_specs=[HBM, VMEM],
        out_specs=[VMEM] * 3,
        scratch_shapes=[pltpu.SemaphoreType.DMA((early_rows // BR,))],
        compiler_params=pltpu.CompilerParams(vmem_limit_bytes=24 << 20),
        cost_estimate=pl.CostEstimate(
            flops=0, bytes_accessed=4 * early_rows * columns * components, transcendentals=0
        ),
        name="early",
    )(pinned[0], border_offsets.T)

    row_filter, col_filter = filter_bands(tile_rows, columns)
    cleaned, late_footprints = pl.pallas_call(
        functools.partial(kernel_background, tile_count),
        out_shape=[
            jax.ShapeDtypeStruct(lined.shape, lined.dtype),
            jax.ShapeDtypeStruct((late_rows, columns, components), footprints.dtype),
        ],
        in_specs=[VMEM] * 4 + [HBM] + [VMEM] * 5,
        out_specs=[VMEM] * 2,
        scratch_shapes=[pltpu.SemaphoreType.DMA((LATE,))],
        compiler_params=pltpu.CompilerParams(vmem_limit_bytes=20 << 20),
        name="background",
    )(
        strip_movie,
        first,
        edge_b,
        edge_a,
        pinned[0],
        border_weight,
        table,
        sides,
        row_filter,
        col_filter,
    )
    split = components // 256 * 256
    height = -(-(components + frames) // 16) * 16
    stacked, coupling, projected = pl.pallas_call(
        functools.partial(kernel_coupling, frames),
        out_shape=[
            jax.ShapeDtypeStruct((height, pixels), jnp.bfloat16),
            jax.ShapeDtypeStruct((components, components), jnp.float32),
            jax.ShapeDtypeStruct((frames, components), jnp.float32),
        ],
        in_specs=[VMEM] * 5,
        out_specs=[VMEM] * 3,
        scratch_shapes=[
            pltpu.VMEM((height, split), jnp.float32),
            pltpu.VMEM((height - split, components - split), jnp.float32),
        ],
        compiler_params=pltpu.CompilerParams(vmem_limit_bytes=24 << 20),
        name="coupling",
    )(early_footprints, late_footprints, kept_footprints, cleaned, support)
    new_traces, rounded, leftover = pl.pallas_call(
        kernel_traces,
        out_shape=[
            jax.ShapeDtypeStruct((frames, components), jnp.float32),
            jax.ShapeDtypeStruct((frames, components), jnp.bfloat16),
            jax.ShapeDtypeStruct((frames, tile_rows, columns), jnp.bfloat16),
        ],
        in_specs=[VMEM] * 5,
        out_specs=[VMEM] * 3,
        scratch_shapes=[lined],
        compiler_params=pltpu.CompilerParams(vmem_limit_bytes=20 << 20),
        name="traces",
    )(stacked, coupling, projected, traces_rows, cleaned)

    frame_count = lax.axis_size("frame")
    all_traces = [rounded] + [
        lax.ppermute(rounded, "frame", pairs(frame_count, turn)) for turn in range(1, frame_count)
    ]
    remainder = lax.all_to_all(leftover, "tile", split_axis=0, concat_axis=0, tiled=True)
    remainder = (
        remainder.reshape(tile_count, own_frames, tile_rows, columns)
        .transpose(1, 0, 2, 3)
        .reshape(own_frames, tile_count * tile_rows, columns)
    )
    trace_gram = pl.pallas_call(
        kernel_gram,
        out_shape=jax.ShapeDtypeStruct((components, components), jnp.float32),
        in_specs=[VMEM] * len(all_traces),
        out_specs=VMEM,
        name="gram",
    )(*all_traces)
    return (new_traces.T, trace_gram, remainder)


def solution(mesh):
    return jax.shard_map(
        per_device,
        mesh=mesh,
        in_specs=(
            P(("frame", "tile"), None, None),
            P("tile", None, None),
            P("tile", None),
            P("tile", "frame"),
            P("tile", None),
            P(),
        ),
        out_specs=(P("tile", "frame"), P("tile", None), P(("frame", "tile"), None, None)),
        check_vma=False,
    )
```

```python
import functools
import math

import jax
import jax.numpy as jnp
import numpy as np
from jax import lax
from jax.experimental import pallas as pl
from jax.experimental.pallas import tpu as pltpu
from jax.sharding import PartitionSpec as P

RR = 16
GR = 4
BR = 8
SWEEPS = 3
NR = 64
HALO = 24
LANES = 128
AHEAD = 3
LATE = 1
VMEM = pl.BlockSpec(memory_space=pltpu.VMEM)
HBM = pl.BlockSpec(memory_space=pltpu.HBM)


def split_high_low(values):
    high = values.astype(jnp.bfloat16)
    low = (values - high.astype(jnp.float32)).astype(jnp.bfloat16)
    return high, low


def filter_bands(tile_rows, columns):
    spots = np.arange(-GR, GR + 1).astype(np.float32)
    raw = np.exp(np.float32(-2.0) * spots * spots / np.float32(GR * GR)).astype(np.float32)
    taps = (raw / raw.sum(dtype=np.float32)).astype(np.float32)

    def band(count_out, count_in, shift):
        distance = np.arange(count_in)[None, :] - np.arange(count_out)[:, None] - shift
        inside = np.abs(distance) <= GR
        return np.where(inside, taps[np.clip(distance + GR, 0, 2 * GR)], np.float32(0.0))

    def parts(matrix):
        high = matrix.astype(jnp.bfloat16)
        low = (matrix - high.astype(np.float32)).astype(jnp.bfloat16)
        return high, low

    rows_high, rows_low = parts(band(tile_rows + 2 * RR, tile_rows + 2 * HALO, HALO - RR))
    cols_high, cols_low = parts(band(columns, columns, 0))
    return (
        jnp.asarray(np.concatenate([rows_high, rows_low], axis=1)),
        jnp.asarray(np.concatenate([cols_high, cols_high, cols_low], axis=0)),
    )


def border_tables(offsets, table_ref, sides_ref):
    columns = table_ref.shape[1]
    tile_rows = sides_ref.shape[0] // 2
    row = offsets[0:1, :]
    col = offsets[1:2, :]
    count = row.shape[1]
    along_top = row == -RR
    along_row = along_top | (row == RR)
    turned_lane = jnp.where(col > 0, columns - col, -col)
    kind = jnp.where(along_row, jnp.where(along_top, 0, 1), jnp.where(col < 0, 2, 3))
    lane = jnp.where(along_row, turned_lane, row + RR)
    kind_hot = jnp.where(kind == lax.broadcasted_iota(jnp.int32, (8, count), 0), 1.0, 0.0)
    lane_hot = jnp.where(lane == lax.broadcasted_iota(jnp.int32, (columns, count), 0), 1.0, 0.0)
    base = lax.dot_general(
        kind_hot.astype(jnp.bfloat16),
        lane_hot.astype(jnp.bfloat16),
        (((1,), (1,)), ((), ())),
        preferred_element_type=jnp.float32,
    )
    distance = lax.broadcasted_iota(jnp.int32, (columns, columns), 0) - lax.broadcasted_iota(
        jnp.int32, (columns, columns), 1
    )
    near = jnp.abs(distance) <= RR
    for kind_at in range(2):
        spread = jnp.broadcast_to(base[kind_at : kind_at + 1, :], (columns, columns))
        turned = pltpu.roll(spread, 0, 1, stride=1, stride_axis=0)
        table_ref[kind_at * columns : (kind_at + 1) * columns, :] = jnp.where(
            near, turned, 0.0
        ).astype(jnp.bfloat16)
    width = sides_ref.shape[1]
    for kind_at in range(2):
        spread = jnp.broadcast_to(base[2 + kind_at : 3 + kind_at, :width], (tile_rows, width))
        turned = pltpu.roll(spread, 0, 1, stride=1, stride_axis=0)
        sides_ref[kind_at * tile_rows : (kind_at + 1) * tile_rows, :] = turned.astype(
            jnp.bfloat16
        )


def block_copies(source, target, arrived, first=0):
    return [
        pltpu.make_async_copy(
            source.at[pl.ds((first + b) * BR, BR)], target.at[pl.ds(b * BR, BR)], arrived.at[b]
        )
        for b in range(target.shape[0] // BR)
    ]


def kernel_fitted(
    footprints_hbm,
    support_hbm,
    traces_hbm,
    fitted_ref,
    kept_ref,
    others_ref,
    support_ref,
    traces_ref,
    lined_ref,
    arrived,
    arrived_small,
):
    small = [
        pltpu.make_async_copy(source, target, arrived_small.at[i])
        for i, (source, target) in enumerate(
            [
                (support_hbm, support_ref),
                (traces_hbm, traces_ref),
            ]
        )
    ]
    for copy in small:
        copy.start()
    tile_rows, columns, components = footprints_hbm.shape
    others = others_ref.shape[0]
    copies = block_copies(footprints_hbm, others_ref, arrived)
    copies.append(
        pltpu.make_async_copy(
            footprints_hbm.at[pl.ds(others, BR)], kept_ref, arrived.at[len(copies)]
        )
    )
    for copy in copies[:AHEAD]:
        copy.start()
    frames = traces_ref.shape[0]
    halves = columns // LANES
    block = BR * columns
    for copy in small:
        copy.wait()
    traces = traces_ref[...]
    for b in range(tile_rows // BR):
        copies[b].wait()
        if b + AHEAD < len(copies):
            copies[b + AHEAD].start()
        raw = kept_ref[...] if b * BR == others else others_ref[b * BR : (b + 1) * BR]
        fitted = lax.dot_general(
            traces * support_ref[b : b + 1, :].astype(jnp.bfloat16),
            raw.reshape(block, components),
            (((1,), (1,)), ((), ())),
            preferred_element_type=jnp.float32,
        )
        for row in range(BR):
            for half in range(halves):
                start = row * columns + half * LANES
                lined_ref[half, pl.ds(b * BR + row, frames, stride=tile_rows), :] = fitted[
                    :, start : start + LANES
                ]
    for half in range(halves):
        for frame in range(frames):
            fitted_ref[frame, :, half * LANES : (half + 1) * LANES] = lined_ref[
                half, frame * tile_rows : (frame + 1) * tile_rows, :
            ]


def kernel_early(footprints_hbm, offsets_ref, early_ref, table_ref, sides_ref, arrived):
    copies = block_copies(footprints_hbm, early_ref, arrived)
    for copy in copies:
        copy.start()
    border_tables(offsets_ref[...], table_ref, sides_ref)
    for copy in copies:
        copy.wait()


def kernel_background(
    tile_count,
    movie_ref,
    first_ref,
    edge_b_ref,
    edge_a_ref,
    footprints_hbm,
    weight_ref,
    table_ref,
    sides_ref,
    row_filter_ref,
    col_filter_ref,
    cleaned_ref,
    late_ref,
    arrived,
):
    frames, tile_rows, columns = movie_ref.shape
    late = tile_rows // BR - 1 - late_ref.shape[0] // BR
    copies = block_copies(footprints_hbm, late_ref, arrived, late)
    for copy in copies:
        copy.start()
    halves = columns // LANES
    span = tile_rows + 2 * RR
    tile = lax.axis_index("tile")
    odd = tile % 2 == 1

    row_number = tile * tile_rows - RR + lax.broadcasted_iota(jnp.int32, (span, 1), 0)
    inside = (row_number >= 0) & (row_number < tile_count * tile_rows)
    row_filter = jnp.where(inside, row_filter_ref[...].astype(jnp.float32), 0.0).astype(
        jnp.bfloat16
    )
    tall = []
    for frame in range(frames):
        edge_a = edge_a_ref[frame].astype(jnp.float32)
        edge_b = edge_b_ref[frame].astype(jnp.float32)
        first = jnp.concatenate(
            [
                jnp.where(odd, edge_a, edge_b),
                first_ref[frame].astype(jnp.float32),
                jnp.where(odd, edge_b, edge_a),
            ],
            axis=0,
        ).astype(jnp.bfloat16)
        tall.append(
            jnp.dot(
                row_filter,
                jnp.concatenate([first, first], axis=0),
                preferred_element_type=jnp.float32,
            )
        )
    high, low = split_high_low(jnp.concatenate(tall, axis=0))
    smooth = jnp.dot(
        jnp.concatenate([high, low, high], axis=1),
        col_filter_ref[...],
        preferred_element_type=jnp.float32,
    ).astype(jnp.bfloat16)
    sides = sides_ref[:, :span]
    lane = lax.broadcasted_iota(jnp.int32, (tile_rows, columns), 1)
    weight = weight_ref[...]
    for frame in range(frames):
        lines = smooth[frame * span : (frame + 1) * span]
        ends = jnp.concatenate([lines[:tile_rows], lines[2 * RR :]], axis=1)
        summed = jnp.dot(ends, table_ref[...], preferred_element_type=jnp.float32)
        mixed = jnp.dot(sides, lines, preferred_element_type=jnp.float32)
        west = pltpu.roll(mixed[:tile_rows], RR, 1)
        east = pltpu.roll(mixed[tile_rows:], columns - RR, 1)
        summed = summed + jnp.where(lane >= RR, west, 0.0)
        summed = summed + jnp.where(lane < columns - RR, east, 0.0)
        background = weight * summed * (1.0 / math.sqrt(NR))
        movie = movie_ref[frame].astype(jnp.float32)
        cleaned = (movie - background).astype(jnp.bfloat16).astype(jnp.float32)
        for half in range(halves):
            cleaned_ref[half, frame * tile_rows : (frame + 1) * tile_rows, :] = cleaned[
                :, half * LANES : (half + 1) * LANES
            ]

    for copy in copies:
        copy.wait()


def kernel_coupling(
    frames,
    early_ref,
    late_ref,
    kept_ref,
    cleaned_ref,
    support_ref,
    stacked_ref,
    coupling_ref,
    projected_ref,
    left_ref,
    right_ref,
):
    columns, components = early_ref.shape[1:]
    parts = [(part, b) for part in (early_ref, late_ref, kept_ref) for b in range(part.shape[0] // BR)]
    tile_rows = len(parts) * BR
    halves = columns // LANES
    block = BR * columns
    split = components // 256 * 256
    spare = stacked_ref.shape[0] - components - frames
    for b in range(tile_rows // BR):
        part, at = parts[b]
        raw = part[at * BR : (at + 1) * BR]
        shaped = raw.reshape(block, components) * support_ref[b : b + 1, :].astype(jnp.bfloat16)
        pixels = slice(b * block, (b + 1) * block)
        stacked_ref[:components, pixels] = shaped.T
        cleaned = jnp.concatenate(
            [
                cleaned_ref[half, pl.ds(row, frames, stride=tile_rows), :]
                for row in range(b * BR, (b + 1) * BR)
                for half in range(halves)
            ],
            axis=1,
        )
        if spare:
            cleaned = jnp.concatenate([cleaned, jnp.zeros((spare, block), jnp.float32)], axis=0)
        stacked_ref[components:, pixels] = cleaned.astype(jnp.bfloat16)
        left = jnp.dot(
            stacked_ref[:, pixels], shaped[:, :split], preferred_element_type=jnp.float32
        )
        right = jnp.dot(
            stacked_ref[split:, pixels], shaped[:, split:], preferred_element_type=jnp.float32
        )
        if b == 0:
            left_ref[...] = left
            right_ref[...] = right
        else:
            left_ref[...] += left
            right_ref[...] += right
    coupling_ref[:, :split] = left_ref[:components]
    coupling_ref[split:, split:] = right_ref[: components - split]
    coupling_ref[:split, split:] = left_ref[split:components].T
    projected_ref[...] = jnp.concatenate(
        [
            left_ref[components : components + frames],
            right_ref[components - split : components - split + frames],
        ],
        axis=1,
    )


def kernel_traces(
    stacked_ref,
    coupling_ref,
    projected_ref,
    traces_ref,
    cleaned_ref,
    new_traces_hbm,
    rounded_ref,
    remainder_hbm,
    refit_ref,
    remainder_ref,
    new_traces_ref,
    left,
):
    frames, tile_rows, columns = remainder_ref.shape
    components = coupling_ref.shape[0]
    halves = columns // LANES
    block = BR * columns
    projected = projected_ref[...]
    coupling = coupling_ref[...]
    diagonal = lax.broadcasted_iota(jnp.int32, coupling.shape, 0) == lax.broadcasted_iota(
        jnp.int32, coupling.shape, 1
    )
    floor = jnp.maximum(
        jnp.sum(jnp.where(diagonal, coupling, 0.0), axis=0, keepdims=True), 1.0
    )
    coupling_high, coupling_low = split_high_low(coupling)
    state = traces_ref[...].astype(jnp.float32)
    for _ in range(SWEEPS):
        state_high, state_low = split_high_low(state)
        by_high = jnp.dot(
            jnp.concatenate([state_high, state_low], axis=0),
            coupling_high,
            preferred_element_type=jnp.float32,
        )
        by_low = jnp.dot(state_high, coupling_low, preferred_element_type=jnp.float32)
        moved = by_high[:frames] + (by_high[frames:] + by_low)
        state = jnp.maximum(state + (projected - moved) / floor, 0.0)
    rounded = state.astype(jnp.bfloat16)
    new_traces_ref[...] = state
    rounded_ref[...] = rounded
    copies = [pltpu.make_async_copy(new_traces_ref, new_traces_hbm, left.at[0])]
    copies[0].start()
    for b in range(tile_rows // BR):
        refit = jnp.dot(
            rounded,
            stacked_ref[:components, b * block : (b + 1) * block],
            preferred_element_type=jnp.float32,
        )
        for row in range(BR):
            for half in range(halves):
                start = row * columns + half * LANES
                refit_ref[half, pl.ds(b * BR + row, frames, stride=tile_rows), :] = refit[
                    :, start : start + LANES
                ]
        if b % 2 == 0:
            continue
        start = (b - 1) * BR
        for frame in range(frames):
            rows = slice(frame * tile_rows + start, frame * tile_rows + start + 2 * BR)
            for half in range(halves):
                remainder_ref[
                    frame, start : start + 2 * BR, half * LANES : (half + 1) * LANES
                ] = (cleaned_ref[half, rows, :] - refit_ref[half, rows, :]).astype(jnp.bfloat16)
        part = pl.ds(start, 2 * BR)
        copies.append(
            pltpu.make_async_copy(
                remainder_ref.at[:, part], remainder_hbm.at[:, part], left.at[len(copies)]
            )
        )
        copies[-1].start()
    for copy in copies:
        copy.wait()


def pairs(count, turn):
    if count & (count - 1):
        return [(i, (i + turn) % count) for i in range(count)]
    return [(i, i ^ turn) for i in range(count)]


def kernel_gram(*refs):
    traces = jnp.concatenate([ref[...] for ref in refs[:-1]], axis=0)
    refs[-1][...] = lax.dot_general(
        traces, traces, (((0,), (0,)), ((), ())), preferred_element_type=jnp.float32
    )


def per_device(movie, footprints, support, traces, border_weight, border_offsets):
    tile_count = lax.axis_size("tile")
    tile_rows, columns, components = footprints.shape
    own_frames = movie.shape[0]
    frames = own_frames * tile_count
    pixels = tile_rows * columns
    halves = columns // LANES
    lined = pltpu.VMEM((halves, frames * tile_rows, LANES), jnp.float32)
    blocks = tile_rows // BR

    pieces = (
        movie.reshape(own_frames, tile_count, tile_rows, columns)
        .transpose(1, 0, 2, 3)
        .reshape(frames, tile_rows, columns)
    )
    strip_movie = lax.all_to_all(pieces, "tile", split_axis=0, concat_axis=0, tiled=True)

    traces_rows = traces.T
    pinned = [
        pltpu.with_memory_space_constraint(array, pltpu.HBM)
        for array in (footprints, support, traces_rows)
    ]
    fitted, kept_footprints = pl.pallas_call(
        kernel_fitted,
        out_shape=[
            jax.ShapeDtypeStruct((frames, tile_rows, columns), jnp.float32),
            jax.ShapeDtypeStruct((BR, columns, components), footprints.dtype),
        ],
        in_specs=[HBM] * 3,
        out_specs=[VMEM] * 2,
        scratch_shapes=[
            pltpu.VMEM((tile_rows - BR, columns, components), footprints.dtype),
            pltpu.VMEM(support.shape, support.dtype),
            pltpu.VMEM(traces_rows.shape, traces.dtype),
            lined,
            pltpu.SemaphoreType.DMA((blocks,)),
            pltpu.SemaphoreType.DMA((2,)),
        ],
        compiler_params=pltpu.CompilerParams(vmem_limit_bytes=24 << 20),
        cost_estimate=pl.CostEstimate(
            flops=2 * frames * pixels * components,
            bytes_accessed=2 * pixels * components,
            transcendentals=0,
        ),
        name="fitted",
    )(*pinned)

    first = (strip_movie.astype(jnp.float32) - fitted).astype(jnp.bfloat16)
    odd = lax.axis_index("tile") % 2 == 1
    top = first[:, :HALO]
    bottom = first[:, tile_rows - HALO :]
    evens = [(i, i + 1) for i in range(0, tile_count - 1, 2)]
    odds = [(i, i + 1) for i in range(1, tile_count - 1, 2)]
    edge_b = lax.ppermute(
        jnp.where(odd, bottom, top), "tile", odds + [(j, i) for i, j in odds]
    )
    edge_a = lax.ppermute(
        jnp.where(odd, top, bottom), "tile", evens + [(j, i) for i, j in evens]
    )

    late_rows = BR * LATE
    early_rows = tile_rows - BR - late_rows
    early_footprints, table, sides = pl.pallas_call(
        kernel_early,
        out_shape=[
            jax.ShapeDtypeStruct((early_rows, columns, components), footprints.dtype),
            jax.ShapeDtypeStruct((2 * columns, columns), jnp.bfloat16),
            jax.ShapeDtypeStruct((2 * tile_rows, LANES), jnp.bfloat16),
        ],
        in_specs=[HBM, VMEM],
        out_specs=[VMEM] * 3,
        scratch_shapes=[pltpu.SemaphoreType.DMA((early_rows // BR,))],
        compiler_params=pltpu.CompilerParams(vmem_limit_bytes=24 << 20),
        cost_estimate=pl.CostEstimate(
            flops=0, bytes_accessed=4 * early_rows * columns * components, transcendentals=0
        ),
        name="early",
    )(pinned[0], border_offsets.T)

    row_filter, col_filter = filter_bands(tile_rows, columns)
    cleaned, late_footprints = pl.pallas_call(
        functools.partial(kernel_background, tile_count),
        out_shape=[
            jax.ShapeDtypeStruct(lined.shape, lined.dtype),
            jax.ShapeDtypeStruct((late_rows, columns, components), footprints.dtype),
        ],
        in_specs=[VMEM] * 4 + [HBM] + [VMEM] * 5,
        out_specs=[VMEM] * 2,
        scratch_shapes=[pltpu.SemaphoreType.DMA((LATE,))],
        compiler_params=pltpu.CompilerParams(vmem_limit_bytes=20 << 20),
        name="background",
    )(
        strip_movie,
        first,
        edge_b,
        edge_a,
        pinned[0],
        border_weight,
        table,
        sides,
        row_filter,
        col_filter,
    )
    split = components // 256 * 256
    height = -(-(components + frames) // 16) * 16
    stacked, coupling, projected = pl.pallas_call(
        functools.partial(kernel_coupling, frames),
        out_shape=[
            jax.ShapeDtypeStruct((height, pixels), jnp.bfloat16),
            jax.ShapeDtypeStruct((components, components), jnp.float32),
            jax.ShapeDtypeStruct((frames, components), jnp.float32),
        ],
        in_specs=[VMEM] * 5,
        out_specs=[VMEM] * 3,
        scratch_shapes=[
            pltpu.VMEM((height, split), jnp.float32),
            pltpu.VMEM((height - split, components - split), jnp.float32),
        ],
        compiler_params=pltpu.CompilerParams(vmem_limit_bytes=24 << 20),
        name="coupling",
    )(early_footprints, late_footprints, kept_footprints, cleaned, support)
    new_traces, rounded, leftover = pl.pallas_call(
        kernel_traces,
        out_shape=[
            jax.ShapeDtypeStruct((frames, components), jnp.float32),
            jax.ShapeDtypeStruct((frames, components), jnp.bfloat16),
            jax.ShapeDtypeStruct((frames, tile_rows, columns), jnp.bfloat16),
        ],
        in_specs=[VMEM] * 5,
        out_specs=[HBM, VMEM, HBM],
        scratch_shapes=[
            lined,
            pltpu.VMEM((frames, tile_rows, columns), jnp.bfloat16),
            pltpu.VMEM((frames, components), jnp.float32),
            pltpu.SemaphoreType.DMA((1 + tile_rows // (2 * BR),)),
        ],
        compiler_params=pltpu.CompilerParams(vmem_limit_bytes=20 << 20),
        name="traces",
    )(stacked, coupling, projected, traces_rows, cleaned)

    frame_count = lax.axis_size("frame")
    all_traces = [rounded] + [
        lax.ppermute(rounded, "frame", pairs(frame_count, turn)) for turn in range(1, frame_count)
    ]
    remainder = lax.all_to_all(leftover, "tile", split_axis=0, concat_axis=0, tiled=True)
    remainder = (
        remainder.reshape(tile_count, own_frames, tile_rows, columns)
        .transpose(1, 0, 2, 3)
        .reshape(own_frames, tile_count * tile_rows, columns)
    )
    trace_gram = pl.pallas_call(
        kernel_gram,
        out_shape=jax.ShapeDtypeStruct((components, components), jnp.float32),
        in_specs=[VMEM] * len(all_traces),
        out_specs=VMEM,
        name="gram",
    )(*all_traces)
    return (new_traces.T, trace_gram, remainder)


def solution(mesh):
    return jax.shard_map(
        per_device,
        mesh=mesh,
        in_specs=(
            P(("frame", "tile"), None, None),
            P("tile", None, None),
            P("tile", None),
            P("tile", "frame"),
            P("tile", None),
            P(),
        ),
        out_specs=(P("tile", "frame"), P("tile", None), P(("frame", "tile"), None, None)),
        check_vma=False,
    )
```
